256 devices in a mesh: dp: 4 (over x), expert: 64 (over y, z, core).
Axes of the slice: x: 4, y: 4, z: 8, core: 2. Of those that a mesh axis runs over, the one named last changes fastest.
Arguments:
- saved_input: bfloat16 [8192, 2048], P(('dp', 'expert')), may hold values from -6 to 6
- output_grad: bfloat16 [8192, 2048], P(('dp', 'expert')), may hold values from -6 to 6
- route_probs: float32 [8192, 8], P(('dp', 'expert')), may hold values from 0.02 to 0.4
- expert_choice: int32 [8192, 8], P(('dp', 'expert')), may hold values from 0 to 127, all different within a row; in each aligned block of 32 rows (0 to 31, 32 to 63, ...) at most 3 rows name the same one
- slot_expert: int32 [4, 64], replicated, may hold values from 0 to 127, as said below
- frozen_gate: bfloat16 [256, 2048, 768], P(('dp', 'expert')), as said below
- frozen_up: bfloat16 [256, 2048, 768], P(('dp', 'expert')), as said below
- frozen_down: bfloat16 [256, 768, 2048], P(('dp', 'expert')), as said below
- adapter_in: float32 [128, 64, 768], P('expert', 'dp'), may hold values from -0.21875 to 0.21875
- adapter_out: float32 [128, 64, 2048], P('expert', 'dp'), may hold values from -0.125 to 0.125
- moment_in: float32 [128, 64, 768], P('expert', 'dp'), may hold values from -3 to 3
- moment_out: float32 [128, 64, 2048], P('expert', 'dp'), may hold values from -3 to 3
- second_in: float32 [128, 64, 768], P('expert', 'dp'), may hold values from 0.01 to 1
- second_out: float32 [128, 64, 2048], P('expert', 'dp'), may hold values from 0.01 to 1
Outputs:
- input_grad: bfloat16 [8192, 2048], P(('dp', 'expert'))
- step_in: float32 [128, 64, 768], P('expert', 'dp')
- step_out: float32 [128, 64, 2048], P('expert', 'dp')
- momentum_in: float32 [128, 64, 768], P('expert', 'dp')
- momentum_out: float32 [128, 64, 2048], P('expert', 'dp')
- variance_in: float32 [128, 64, 768], P('expert', 'dp')
- variance_out: float32 [128, 64, 2048], P('expert', 'dp')
- replica_in: bfloat16 [256, 64, 768], P(('dp', 'expert'))
- replica_out: bfloat16 [256, 64, 2048], P(('dp', 'expert'))
The draws below stay inside these ranges and needn't reach their ends.
Inputs may be any that keep to these rules, and one draw needn't show every extreme that they name: `expert_choice`: among the rows of one device no expert is named more than 3 times. `slot_expert`: the slots of index j of the expert axis host only experts 2 * j to 2 * j + 1, and each of these at least once. `frozen_gate`: slots that host the same expert hold the same frozen weights. `frozen_up`: slots that host the same expert hold the same frozen weights. `frozen_down`: slots that host the same expert hold the same frozen weights.
All inputs are finite; a program needn't handle non-finite values.
Results may differ from the reference program's by a relative error of at most 0.012.
Values may be sent and summed in bfloat16 or wider, within the bound.
A program may use at most 128 MiB of HBM per device.

```python
import math
import jax
import jax.numpy as jnp
import numpy as np
from jax import lax

D = 2048
H = 768
TOPK = 8
R = 64
EXP_COL = 2
STEP = 100
TOK_DEV = 32
EXPERTS = 128
SLOTS = 256
TOKENS = 8192
CAP = 3
N_DP = 4
N_EXPERT = 64


def slot_table(key):
    salted = jax.random.fold_in(key, 7)
    first_key, second_key = jax.random.split(salted)
    extra = jax.random.randint(first_key, (N_EXPERT, N_DP), 0, EXP_COL)
    places = jnp.arange(N_DP, dtype=jnp.int32)
    local = jnp.where(places[None, :] < EXP_COL, places[None, :], extra)
    column_keys = jax.random.split(second_key, N_EXPERT)
    shuffle = jax.vmap(lambda inner_key: jax.random.permutation(inner_key, N_DP))(column_keys)
    mixed = jnp.take_along_axis(local, shuffle, axis=1)
    hosting = mixed + EXP_COL * jnp.arange(N_EXPERT, dtype=jnp.int32)[:, None]
    return hosting.T.astype(jnp.int32)


def expert_weights(key, salt, height, breadth, fan_in):
    hosting = slot_table(key).reshape(-1)
    salted = jax.random.fold_in(key, salt)

    def per_slot(expert):
        values = jax.random.truncated_normal(jax.random.fold_in(salted, expert), -4.0, 4.0, (height, breadth), jnp.float32)
        return (values * fan_in ** (-0.5)).astype(jnp.bfloat16)
    return jax.lax.map(per_slot, hosting)


def draw_slot_expert(key, part):
    return slot_table(key)


def draw_frozen_gate(key, part):
    return expert_weights(key, 101, D, H, D)


def draw_frozen_up(key, part):
    return expert_weights(key, 202, D, H, D)


def draw_frozen_down(key, part):
    return expert_weights(key, 303, H, D, H)


def steps_of(stream_key, extent, cuts, low, largest):
    def one(dim, parts):
        heights = jax.random.uniform(jax.random.fold_in(jax.random.fold_in(stream_key, 6), dim), (parts,), jnp.float32, low / len(cuts), largest / len(cuts))
        return jnp.repeat(jnp.exp(heights), extent[dim] // parts).reshape((-1,) + (1,) * (len(extent) - dim - 1))

    level = one(*cuts[0])
    for cut in cuts[1:]:
        level = level * one(*cut)
    return level


def assign_block(rng, own, number, rows, number_of, top, reach, slope):
    sequence = jax.random.permutation(rng, number_of)
    crowded, usual = portions_of(number_of, rows * top, reach, slope, True), portions_of(number_of, rows * top, reach, slope, False)
    places = jnp.arange(number_of)

    def named(sizes, offset_by):
        used = int((sizes > 0).sum())
        fixed = max(1, used // 4)
        shifted = fixed + (places - fixed + offset_by * (used - fixed)) % max(1, number_of - fixed)
        return jnp.zeros((number_of,), jnp.int32).at[sequence[jnp.where(places < fixed, places, shifted)]].set(jnp.asarray(sizes, jnp.int32))

    sizes = jnp.where(number % 4 == 0, named(crowded, number // 4), named(usual, number - number // 4 - 1))
    mixed = jax.random.permutation(jax.random.fold_in(own, 3), number_of)
    source_of, taker = mixed[0:number_of // 2 * 2:2], mixed[1:number_of // 2 * 2:2]
    margin = jnp.minimum(sizes[source_of] - 1, reach - sizes[taker]) // 2
    margin = jnp.where((source_of == sequence[0]) | (taker == sequence[0]) | (sizes[taker] == 0), 0, jnp.maximum(margin, 0))
    shifted = jax.random.randint(jax.random.fold_in(own, 4), (number_of // 2,), 0, 1 << 20) % (margin + 1)
    sizes = sizes.at[source_of].add(-shifted).at[taker].add(shifted)
    members = jnp.searchsorted(jnp.cumsum(sizes), jnp.arange(rows * top), side="right").astype(jnp.int32)
    grid = members.reshape(top, rows).T
    grid = grid[jax.random.permutation(jax.random.fold_in(own, 1), rows)]
    offset_by = jax.random.randint(jax.random.fold_in(own, 2), (rows, 1), 0, top)
    return jnp.take_along_axis(grid, (jnp.arange(top)[None, :] + offset_by) % top, axis=1)


def portions_of(count, total, reach, lean, full):
    portions = [(1 << 20) // math.isqrt(standing ** lean) + 1 for standing in range(1, count + 1)]
    largest = reach if full else min(reach, max(-(-total // count), total * portions[0] // sum(portions)))
    least = 1 if total - largest >= count - 1 else 0
    given, surplus = [largest] + [least] * (count - 1), total - largest - least * (count - 1)
    while surplus > 0:
        candidates = [i for i in range(1, count) if given[i] < largest] or [i for i in range(1, count) if given[i] < reach]
        pool, remaining = sum([portions[i] for i in candidates]), surplus
        for i in candidates:
            more = min(reach - given[i], max(1, remaining * portions[i] // pool), surplus)
            given[i] = given[i] + more
            surplus = surplus - more
    return np.array(given)


def scatter_about(stream_key, dims, scale, limit, pieces=(), kind=jnp.bfloat16):
    loudness = steps_of(stream_key, dims, pieces, -0.22, 0.18) if pieces else 1.0
    array = jax.random.normal(stream_key, dims, jnp.float32) * scale * loudness
    return jnp.minimum(jnp.maximum(array, -limit), limit).astype(kind)


def setup_inputs(seed: int = 0) -> dict:
    streams_of = jax.random.split(jax.random.key(seed), 15)
    saved_input = scatter_about(streams_of[0], (TOKENS, D), 1.0, 6.0, ((0, 256),))
    output_grad = scatter_about(streams_of[1], (TOKENS, D), 1.0, 6.0, ((0, 256),))
    route_probs = jnp.clip(0.02 + 0.38 * jax.random.uniform(streams_of[2], (TOKENS, TOPK), jnp.float32) ** steps_of(streams_of[2], (TOKENS, TOPK), ((0, 256),), -0.2, 0.2), 0.02, 0.4)
    expert_choice_keys = jax.random.split(jax.random.fold_in(streams_of[3], 1), TOKENS // TOK_DEV)
    expert_choice_turns = jax.random.permutation(jax.random.fold_in(streams_of[3], 3), TOKENS // TOK_DEV)
    expert_choice = jax.vmap(lambda own, number: assign_block(jax.random.fold_in(streams_of[3], 2), own, number, TOK_DEV, EXPERTS, TOPK, CAP, 2))(expert_choice_keys, expert_choice_turns).reshape((TOKENS, TOPK))
    slot_expert = draw_slot_expert(jax.random.fold_in(streams_of[14], 71), 0)
    frozen_gate = draw_frozen_gate(jax.random.fold_in(streams_of[14], 71), 0)
    frozen_up = draw_frozen_up(jax.random.fold_in(streams_of[14], 71), 0)
    frozen_down = draw_frozen_down(jax.random.fold_in(streams_of[14], 71), 0)
    adapter_in = scatter_about(streams_of[8], (EXPERTS, R, H), H ** -0.5, 0.21875, ((0, 64), (1, 4)), jnp.float32)
    adapter_out = scatter_about(streams_of[9], (EXPERTS, R, D), D ** -0.5, 0.125, ((0, 64), (1, 4)), jnp.float32)
    moment_in = scatter_about(streams_of[10], (EXPERTS, R, H), 0.3, 3.0, ((0, 64), (1, 4)), jnp.float32)
    moment_out = scatter_about(streams_of[11], (EXPERTS, R, D), 0.3, 3.0, ((0, 64), (1, 4)), jnp.float32)
    second_in = jnp.clip(jnp.exp(math.log(1.0) - 4.6051702 * jax.random.uniform(streams_of[12], (EXPERTS, R, H), jnp.float32) ** steps_of(streams_of[12], (EXPERTS, R, H), ((0, 64), (1, 4)), -0.2, 0.2)), 0.01, 1.0)
    second_out = jnp.clip(jnp.exp(math.log(1.0) - 4.6051702 * jax.random.uniform(streams_of[13], (EXPERTS, R, D), jnp.float32) ** steps_of(streams_of[13], (EXPERTS, R, D), ((0, 64), (1, 4)), -0.2, 0.2)), 0.01, 1.0)
    return dict(saved_input=saved_input, output_grad=output_grad, route_probs=route_probs, expert_choice=expert_choice, slot_expert=slot_expert, frozen_gate=frozen_gate, frozen_up=frozen_up, frozen_down=frozen_down, adapter_in=adapter_in, adapter_out=adapter_out, moment_in=moment_in, moment_out=moment_out, second_in=second_in, second_out=second_out)


adapter_scale_factor = 2.0
beta_one = 0.9
beta_two = 0.999
decay_rate = 0.01
adam_eps = 1e-08

def route_all(expert_choice, slot_expert):
    row_count = TOKENS * TOPK
    flat = expert_choice.reshape(row_count).astype(jnp.int32)
    row_ids = jnp.arange(row_count, dtype=jnp.int32)
    source = row_ids // (TOK_DEV * TOPK)
    column = flat // EXP_COL
    hosted = (slot_expert[:, column] == flat[None, :]).astype(jnp.int32)
    counts = lax.optimization_barrier(jnp.sum(hosted, axis=0))
    picked = source % counts
    running = jnp.cumsum(hosted, axis=0) - 1
    chosen = hosted * (running == picked[None, :]).astype(jnp.int32)
    dest_row = lax.optimization_barrier(jnp.sum(chosen * jnp.arange(N_DP, dtype=jnp.int32)[:, None], axis=0))
    blocks = flat.reshape(SLOTS, TOK_DEV * TOPK)
    inner = jnp.arange(TOK_DEV * TOPK, dtype=jnp.int32)
    earlier = (blocks[:, None, :] == blocks[:, :, None]) & (inner[None, None, :] < inner[None, :, None])
    rank = lax.optimization_barrier(jnp.sum(earlier.astype(jnp.int32), axis=2)).reshape(row_count)
    slot = dest_row * N_EXPERT + column
    return (slot * SLOTS + source) * CAP + rank

def expert_backward(buffer_rows, gradient_row_block, gate_weight, up_weight, down_weight, owned_input, own_out):
    gate_pre = jnp.dot(buffer_rows, gate_weight, preferred_element_type=jnp.float32)
    up_pre = jnp.dot(buffer_rows, up_weight, preferred_element_type=jnp.float32)
    sigmoid_gate = jax.nn.sigmoid(gate_pre)
    hidden_state = (gate_pre * sigmoid_gate * up_pre).astype(jnp.bfloat16)
    low_rank_input = jnp.dot(hidden_state, owned_input.T, preferred_element_type=jnp.float32).astype(jnp.bfloat16)
    low_rank_gradient = jnp.dot(gradient_row_block, own_out.T, preferred_element_type=jnp.float32).astype(jnp.bfloat16)
    hidden_gradient = jnp.dot(gradient_row_block, down_weight.T, preferred_element_type=jnp.float32)
    hidden_gradient = hidden_gradient + adapter_scale_factor * jnp.dot(low_rank_gradient, owned_input, preferred_element_type=jnp.float32)
    up_grad = (hidden_gradient * gate_pre * sigmoid_gate).astype(jnp.bfloat16)
    gate_grad = (hidden_gradient * up_pre * sigmoid_gate * (1.0 + gate_pre * (1.0 - sigmoid_gate))).astype(jnp.bfloat16)
    back_rows = jnp.dot(gate_grad, gate_weight.T, preferred_element_type=jnp.float32)
    back_rows = (back_rows + jnp.dot(up_grad, up_weight.T, preferred_element_type=jnp.float32)).astype(jnp.bfloat16)
    incoming_gradient = adapter_scale_factor * jnp.dot(low_rank_gradient.T, hidden_state, preferred_element_type=jnp.float32)
    outgoing_gradient = adapter_scale_factor * jnp.dot(low_rank_input.T, gradient_row_block, preferred_element_type=jnp.float32)
    return (back_rows, incoming_gradient, outgoing_gradient)

def adamw(param, grad, first, second):
    first_new = beta_one * first + (1.0 - beta_one) * grad
    second_new = beta_two * second + (1.0 - beta_two) * grad * grad
    corr_one = 1.0 - beta_one ** STEP
    corr_two = 1.0 - beta_two ** STEP
    step_dir = first_new / corr_one / (jnp.sqrt(second_new / corr_two) + adam_eps) + decay_rate * param
    return (step_dir, first_new, second_new)

def reference(saved_input, output_grad, route_probs, expert_choice, slot_expert, frozen_gate, frozen_up, frozen_down, adapter_in, adapter_out, moment_in, moment_out, second_in, second_out):
    row_count = TOKENS * TOPK
    position = route_all(expert_choice, slot_expert)
    row_ids = jnp.arange(row_count, dtype=jnp.int32)
    block_rows = SLOTS * CAP
    filler = jnp.full((SLOTS * block_rows,), row_count, jnp.int32).at[position].set(row_ids)
    scaled = (route_probs[:, :, None] * output_grad[:, None, :].astype(jnp.float32)).astype(jnp.bfloat16).reshape(row_count, D)
    hosting = slot_expert.reshape(SLOTS).astype(jnp.int32)

    def one_slot(carry, slot):
        grad_acc, sum_in, sum_out = carry
        picked = lax.dynamic_slice_in_dim(filler, slot * block_rows, block_rows)
        token_idx = picked // TOPK
        buffer_rows = jnp.take(saved_input, token_idx, axis=0, mode='fill', fill_value=0)
        gradient_row_block = jnp.take(scaled, picked, axis=0, mode='fill', fill_value=0)
        expert = hosting[slot]
        owned_input = adapter_in[expert].astype(jnp.bfloat16)
        own_out = adapter_out[expert].astype(jnp.bfloat16)
        back_rows, incoming_gradient, outgoing_gradient = expert_backward(buffer_rows, gradient_row_block, frozen_gate[slot], frozen_up[slot], frozen_down[slot], owned_input, own_out)
        grad_acc = grad_acc.at[token_idx].add(back_rows.astype(jnp.float32), mode='drop')
        sum_in = sum_in.at[expert].add(incoming_gradient)
        sum_out = sum_out.at[expert].add(outgoing_gradient)
        return ((grad_acc, sum_in, sum_out), None)
    start = (jnp.zeros((TOKENS, D), jnp.float32), jnp.zeros((EXPERTS, R, H), jnp.float32), jnp.zeros((EXPERTS, R, D), jnp.float32))
    (grad_acc, sum_in, sum_out), _ = lax.scan(one_slot, start, jnp.arange(SLOTS, dtype=jnp.int32))
    input_grad = grad_acc.astype(jnp.bfloat16)
    step_in, momentum_in, variance_in = adamw(adapter_in, sum_in, moment_in, second_in)
    step_out, momentum_out, variance_out = adamw(adapter_out, sum_out, moment_out, second_out)
    replica_in = step_in.astype(jnp.bfloat16)[hosting]
    replica_out = step_out.astype(jnp.bfloat16)[hosting]
    return (input_grad, step_in, step_out, momentum_in, momentum_out, variance_in, variance_out, replica_in, replica_out)
```

```python
import functools

import jax
import jax.numpy as jnp
from jax import lax
from jax.experimental import pallas as pl
from jax.experimental.pallas import tpu as pltpu
from jax.sharding import PartitionSpec as P

MESH = pl.DeviceIdType.MESH
STEP = 100
SCALE = 2.0
BETA1 = 0.9
BETA2 = 0.999
DECAY = 0.01
EPS = 1e-08
ND, NY, NZ = 4, 4, 8
CAP = 3
NS = 2 * NZ
ROWS = CAP * NS
PLANE = NY * ROWS
ALL_ROWS = ND * PLANE
HALF = NZ // 2
NC = 4
BF = jnp.bfloat16
F32 = jnp.float32


def dot(a, b, dims=((1,), (0,))):
    return lax.dot_general(a, b, (dims, ((), ())), preferred_element_type=F32)


def choose(flag, a, b):
    return jnp.where(jnp.full(a.shape, flag, F32) > 0.5, a, b)


def adamw(param, grad, first, second):
    first_new = BETA1 * first + (1.0 - BETA1) * grad
    second_new = BETA2 * second + (1.0 - BETA2) * grad * grad
    corr_one = 1.0 - BETA1**STEP
    corr_two = 1.0 - BETA2**STEP
    step = first_new / corr_one / (jnp.sqrt(second_new / corr_two) + EPS) + DECAY * param
    return step, first_new, second_new


def kernel(
    x_ref, g_ref, meta_ref, slots_ref, wg_hbm, wu_hbm, wd_hbm, *rest
):
    adam_hbm, rest = rest[:6], rest[6:]
    (ig_out, st_in, st_out, mo_in, mo_out, va_in, va_out, re_in, re_out), rest = rest[:9], rest[9:]
    (
        wg, wu, wd, adam_in, adam_out, stage, zbuf, mbuf, pick, pick_t, weight, sendbuf, obuf, xbuf,
        gacc, uacc, hacc, lacc, hid, ugr, ggr, lgr, lin,
        bbuf, r1buf, r2buf, osum, rbuf, tok, zs1, zr1, zsn, zrn, fin, ig,
        ad_in, ad_out, cin, cout, gs_in, gs_out, gr_in, gr_out, ss_in, ss_out, rin, rout,
        hbm_sem, sib_s, sib_r, z_s, z_r, y_s, y_r, yl_s, x_s, x_r, a_s, a_r,
        b1_s, b1_r, b2_s, b2_r, q_s, q_r, ql_s, t_s, t_r, f_s, f_r, g_s, g_r, s_s, s_r,
    ) = rest
    D, H = wg.shape
    T = x_ref.shape[0]
    R = cin.shape[0] * cin.shape[1]
    CC = D // NC
    CH = CC // 2
    d = lax.axis_index("dp")
    j = lax.axis_index("expert")
    y = lax.div(j, 2 * NZ)
    z = lax.rem(lax.div(j, 2), NZ)
    k = lax.rem(j, 2)
    ok = 1 - k

    def col(yy, zz, kk):
        return (yy * NZ + zz) * 2 + kk

    def ymod(o):
        return lax.rem(y + o + NY, NY)

    def zmod(o):
        return lax.rem(z + o + NZ, NZ)

    def xmod(o):
        return lax.rem(d + o + ND, ND)

    sibling = (d, col(y, z, ok))
    up_z, down_z = (d, col(y, zmod(1), k)), (d, col(y, zmod(-1), k))
    right, left = (xmod(1), j), (xmod(-1), j)

    sent = []

    def send(src, dst, ss, rs, dev):
        c = pltpu.make_async_remote_copy(
            src_ref=src, dst_ref=dst, send_sem=ss, recv_sem=rs, device_id=dev, device_id_type=MESH
        )
        c.start()
        sent.append(c)

    def landed(dst, rs):
        pltpu.make_async_remote_copy(
            src_ref=dst, dst_ref=dst, send_sem=rs, recv_sem=rs, device_id=sibling, device_id_type=MESH
        ).wait_recv()

    loads = [
        pltpu.make_async_copy(wg_hbm.at[0], wg, hbm_sem.at[0]),
        pltpu.make_async_copy(wu_hbm.at[0], wu, hbm_sem.at[1]),
        pltpu.make_async_copy(wd_hbm.at[0], wd, hbm_sem.at[2]),
    ]
    adam_loads = []
    for i in range(3):
        adam_loads.append(pltpu.make_async_copy(adam_hbm[2 * i], adam_in.at[i], hbm_sem.at[3 + 2 * i]))
        adam_loads.append(pltpu.make_async_copy(adam_hbm[2 * i + 1], adam_out.at[i], hbm_sem.at[4 + 2 * i]))
    for c in adam_loads + loads:
        c.start()

    partners = [sibling, up_z, down_z]
    partners += [(d, col(ymod(o), z, kk)) for o in range(1, NY) for kk in range(2)]
    partners += [(xmod(o), j) for o in range(1, ND)]
    barrier = pltpu.get_barrier_semaphore()
    for dev in partners:
        pl.semaphore_signal(barrier, inc=1, device_id=dev, device_id_type=MESH)

    @pl.when(k == 0)
    def _():
        for c in range(NC):
            zbuf[c, z, 0] = x_ref[:, c * CC : (c + 1) * CC]
            stage[c] = g_ref[:, c * CC : (c + 1) * CC]

    @pl.when(k == 1)
    def _():
        for c in range(NC):
            zbuf[c, z, 1] = g_ref[:, c * CC : (c + 1) * CC]
            stage[c] = x_ref[:, c * CC : (c + 1) * CC]

    mbuf[z, k] = meta_ref[...]
    pl.semaphore_wait(barrier, len(partners))

    send(meta_ref, mbuf.at[z, k], sib_s.at[NC], sib_r.at[NC], sibling)
    for c in range(NC):
        send(stage.at[c], zbuf.at[c, z, k], sib_s.at[c], sib_r.at[c], sibling)

    def zref(c):
        return mbuf if c == NC else zbuf.at[c]

    def z_send(c, i):
        buf = zref(c)
        a, b = zmod(1 - i), zmod(i - 1)
        if i < HALF:
            send(buf.at[a], buf.at[a], z_s.at[c, 0, i - 1], z_r.at[c, 0, i - 1], up_z)
            send(buf.at[b], buf.at[b], z_s.at[c, 1, i - 1], z_r.at[c, 1, i - 1], down_z)
        else:
            send(buf.at[a, 0], buf.at[a, 0], z_s.at[c, 0, i - 1], z_r.at[c, 0, i - 1], up_z)
            send(buf.at[b, 1], buf.at[b, 1], z_s.at[c, 1, i - 1], z_r.at[c, 1, i - 1], down_z)

    def z_wait(c, i):
        buf = zref(c)
        a, b = zmod(-i), zmod(i)
        if i < HALF:
            landed(buf.at[a], z_r.at[c, 0, i - 1])
            landed(buf.at[b], z_r.at[c, 1, i - 1])
        else:
            landed(buf.at[a, 0], z_r.at[c, 0, i - 1])
            landed(buf.at[b, 1], z_r.at[c, 1, i - 1])

    def z_step(c, i):
        if i == 0:
            landed(zref(c).at[z, ok], sib_r.at[c])
        else:
            z_wait(c, i)
        if i < HALF:
            z_send(c, i + 1)

    def slot(q, jj):
        return slots_ref[q, jj].astype(F32)

    hosted = slot(d, j)
    first = (2 * j).astype(F32)
    both = (4 * j + 1).astype(F32)

    taken = jnp.float32(1.0)
    for q in range(ND):
        same = jnp.where(slot(q, j) == hosted, 1.0, 0.0)
        taken = taken * jnp.where(q < d, 1.0 - same, 1.0)
    mine = [jnp.float32(1.0)] + [
        taken * jnp.where(both - slot(xmod(-o), j) == hosted, 1.0, 0.0) for o in range(1, ND)
    ]

    def build_pick():
        groups = [
            mbuf[2 * q, 0] + mbuf[2 * q, 1] + mbuf[2 * q + 1, 0] + mbuf[2 * q + 1, 1]
            for q in range(NZ // 2)
        ]
        meta = jnp.concatenate(groups, axis=1)
        width = meta.shape[1]
        row = lax.broadcasted_iota(jnp.int32, (NS, width), 0)
        lane = lax.broadcasted_iota(jnp.int32, (NS, width), 1)
        experts = jnp.zeros((NS, width), F32)
        for o in range(NY):
            for kk in range(2):
                jj = col(ymod(o), z, kk)
                host = slot(d, jj)
                other = (4 * jj + 1).astype(F32) - host
                e = (o * 2 + kk) * 2
                experts = jnp.where(row == e, jnp.full((NS, width), host, F32), experts)
                experts = jnp.where(row == e + 1, jnp.full((NS, width), other, F32), experts)
        hit = jnp.zeros((NS, width), F32)
        prob = jnp.zeros((NS, width), F32)
        for kk in range(8):
            m = jnp.broadcast_to(meta[kk : kk + 1], (NS, width)) == experts
            hit = jnp.where(m, 1.0, hit)
            prob = jnp.where(m, jnp.broadcast_to(meta[8 + kk : 9 + kk], (NS, width)), prob)
        seg = lax.shift_right_logical(lane, 5) == row
        sa = lax.broadcasted_iota(jnp.int32, (width, width), 0)
        sb = lax.broadcasted_iota(jnp.int32, (width, width), 1)
        before = (sa < sb) & (lax.shift_right_logical(sa, 5) == lax.shift_right_logical(sb, 5))
        rank = dot(hit.astype(BF), jnp.where(before, 1.0, 0.0).astype(BF))
        key = jnp.where(hit > 0.5, rank, -1.0)
        unit = jnp.where(k == 0, 1.0, 0.0)
        for e in range(4 * NY):
            for r in range(CAP):
                at = (e * CAP + r) * NS
                m = (jnp.broadcast_to(key[e : e + 1], (NS, width)) == float(r)) & seg
                block = jnp.where(m, 1.0, 0.0)
                pick[pl.ds(at, NS), :] = block.astype(BF)
                total = jnp.sum(block * jnp.broadcast_to(prob[e : e + 1], (NS, width)), axis=1, keepdims=True)
                total = unit + (1.0 - unit) * total
                weight[pl.ds(at, NS), :] = jnp.broadcast_to(total, (NS, weight.shape[1]))

    def select(c):
        tokens = zbuf[c].reshape(NS * T, CC)
        for o in (2, 1, 3, 0):
            for kk in range(2):
                t = o * 2 + kk
                rows = pl.ds(t * 2 * ROWS, 2 * ROWS)
                got = dot(pick[rows, :], tokens)
                w = weight[rows, :]
                got = jnp.concatenate([got[:, i : i + 128] * w for i in range(0, CC, 128)], axis=1)
                sendbuf[c, t] = got.astype(BF).reshape(2, ROWS, CC)
                if o:
                    dev = (d, col(ymod(o), z, kk))
                    send(sendbuf.at[c, t, 0], xbuf.at[c, k, 0, o], y_s.at[c, t, 0], y_r.at[c, o, k, 0], dev)
                    send(sendbuf.at[c, t, 1], obuf.at[c, k, o], y_s.at[c, t, 1], y_r.at[c, o, k, 1], dev)
        send(sendbuf.at[c, ok, 0], xbuf.at[c, k, 0, 0], y_s.at[c, 0, 0], y_r.at[c, 0, k, 0], sibling)
        send(sendbuf.at[c, ok, 1], obuf.at[c, k, 0], y_s.at[c, 0, 1], y_r.at[c, 0, k, 1], sibling)
        own = [
            pltpu.make_async_copy(sendbuf.at[c, k, 0], xbuf.at[c, k, 0, 0], yl_s.at[c, 0]),
            pltpu.make_async_copy(sendbuf.at[c, k, 1], obuf.at[c, k, 0], yl_s.at[c, 1]),
        ]
        for copy in own:
            copy.start()
        return own

    def y_wait(c, own):
        for o in range(1, NY):
            for kk in range(2):
                landed(obuf.at[c, kk, o], y_r.at[c, o, kk, 1])
        landed(obuf.at[c, ok, 0], y_r.at[c, 0, ok, 1])
        own[1].wait()
        send(obuf.at[c], xbuf.at[c, :, 1], x_s.at[c, 0], x_r.at[c, 0], right)
        send(obuf.at[c], xbuf.at[c, :, 3], x_s.at[c, 1], x_r.at[c, 1], left)
        for o in range(1, NY):
            for kk in range(2):
                landed(xbuf.at[c, kk, 0, o], y_r.at[c, o, kk, 0])
        landed(xbuf.at[c, ok, 0, 0], y_r.at[c, 0, ok, 0])
        own[0].wait()

    def x_forward(c):
        landed(xbuf.at[c, :, 1], x_r.at[c, 0])
        landed(xbuf.at[c, :, 3], x_r.at[c, 1])
        send(xbuf.at[c, 0, 1], xbuf.at[c, 0, 2], x_s.at[c, 2], x_r.at[c, 2], right)
        send(xbuf.at[c, 1, 3], xbuf.at[c, 1, 2], x_s.at[c, 3], x_r.at[c, 3], left)

    def x_wait(c):
        landed(xbuf.at[c, 0, 2], x_r.at[c, 2])
        landed(xbuf.at[c, 1, 2], x_r.at[c, 3])

    NB = 256

    def accumulate(c):
        def add(acc, cols, value):
            n = value.shape[1]
            for p in range(ND):
                rows = slice(p * PLANE, (p + 1) * PLANE)
                part = value[rows]
                if p:
                    part = choose(mine[p], part, jnp.zeros((PLANE, n), F32))
                if c == 0:
                    acc[rows, cols] = part
                else:
                    acc[rows, cols] += part

        def body(n, carry):
            cols = pl.ds(pl.multiple_of(n * NB, NB), NB)
            rows_x = xbuf[c, 0].reshape(ALL_ROWS, CC)
            add(gacc, cols, dot(rows_x, wg[c * CC : (c + 1) * CC, cols]))
            add(uacc, cols, dot(rows_x, wu[c * CC : (c + 1) * CC, cols]))
            rows_g = xbuf[c, 1].reshape(ALL_ROWS, CC)
            add(hacc, cols, dot(rows_g, wd[cols, c * CC : (c + 1) * CC], ((1,), (1,))))
            return carry

        lax.fori_loop(0, H // NB, body, 0)
        rows_g = xbuf[c, 1].reshape(ALL_ROWS, CC)
        co = cout[:, :, c * CC : (c + 1) * CC].reshape(R, CC)
        add(lacc, slice(0, R), dot(rows_g, co, ((1,), (1,))))

    EB = 96

    def middle():
        ci = cin[...].reshape(R, H)

        def body(n, carry):
            rows = pl.ds(pl.multiple_of(n * EB, EB), EB)
            low = lacc[rows, :].astype(BF)
            lgr[rows, :] = low
            gate, up = gacc[rows, :], uacc[rows, :]
            hg = hacc[rows, :] + SCALE * dot(low, ci)
            sg = jax.nn.sigmoid(gate)
            act = gate * sg
            hidden = (act * up).astype(BF)
            hid[rows, :] = hidden
            ugr[rows, :] = (hg * act).astype(BF)
            ggr[rows, :] = (hg * up * sg * (1.0 + gate * (1.0 - sg))).astype(BF)
            lin[rows, :] = dot(hidden, ci, ((1,), (1,))).astype(BF)
            return carry

        lax.fori_loop(0, ALL_ROWS // EB, body, 0)

    def back(c):
        for h in range(2):
            lo = c * CC + h * CH
            r = dot(ggr[...], wg[lo : lo + CH, :], ((1,), (1,))) + dot(ugr[...], wu[lo : lo + CH, :], ((1,), (1,)))
            r = r.astype(BF).reshape(ND, NY, ROWS, CH)
            for p in range(ND):
                bbuf[c, p, h] = r[p]
        send(bbuf.at[c, 2, 0], r1buf.at[c, 0], b1_s.at[c, 0], b1_r.at[c, 0], right)
        send(bbuf.at[c, 2, 1], r1buf.at[c, 1], b1_s.at[c, 1], b1_r.at[c, 1], left)

    def back_forward(c):
        landed(r1buf.at[c, 0], b1_r.at[c, 0])
        bbuf[c, 3, 0] = bbuf[c, 3, 0] + r1buf[c, 0]
        send(bbuf.at[c, 3], r2buf.at[c, 0], b2_s.at[c, 0], b2_r.at[c, 0], right)
        landed(r1buf.at[c, 1], b1_r.at[c, 1])
        bbuf[c, 1, 1] = bbuf[c, 1, 1] + r1buf[c, 1]
        send(bbuf.at[c, 1], r2buf.at[c, 1], b2_s.at[c, 1], b2_r.at[c, 1], left)

    def y_back(c):
        for o in (2, 1, 3):
            for h in range(2):
                dev = (d, col(ymod(-o), z, h))
                send(bbuf.at[c, 0, h, o], rbuf.at[c, o * 2 + k, 0], q_s.at[c, o, h, 0], q_r.at[c, o, k, 0], dev)
        send(bbuf.at[c, 0, ok, 0], rbuf.at[c, k, 0], q_s.at[c, 0, 0, 0], q_r.at[c, 0, k, 0], sibling)
        own = [pltpu.make_async_copy(bbuf.at[c, 0, k, 0], rbuf.at[c, k, 0], ql_s.at[c, 0])]
        own[0].start()
        landed(r2buf.at[c, 0], b2_r.at[c, 0])
        landed(r2buf.at[c, 1], b2_r.at[c, 1])
        osum[c] = r2buf[c, 0] + r2buf[c, 1]
        for o in (2, 1, 3):
            for h in range(2):
                dev = (d, col(ymod(-o), z, h))
                send(osum.at[c, h, o], rbuf.at[c, o * 2 + k, 1], q_s.at[c, o, h, 1], q_r.at[c, o, k, 1], dev)
        send(osum.at[c, ok, 0], rbuf.at[c, k, 1], q_s.at[c, 0, 0, 1], q_r.at[c, 0, k, 1], sibling)
        own.append(pltpu.make_async_copy(osum.at[c, k, 0], rbuf.at[c, k, 1], ql_s.at[c, 1]))
        own[1].start()
        return own

    def tokens_back(c, own):
        for i in range(2):
            for o in range(1, NY):
                for kk in range(2):
                    landed(rbuf.at[c, o * 2 + kk, i], q_r.at[c, o, kk, i])
            landed(rbuf.at[c, ok, i], q_r.at[c, 0, ok, i])
            own[i].wait()
        got = dot(pick_t[...], rbuf[c].reshape(ALL_ROWS, CH))
        tok[c] = got.reshape(NZ, 2, T, CH)
        zs1[c, 0] = tok[c, zmod(HALF), 0].astype(BF)
        zs1[c, 1] = tok[c, zmod(-HALF), 1].astype(BF)
        send(zs1.at[c, 0], zr1.at[c, 0], t_s.at[c, 0, 0], t_r.at[c, 0, 0], up_z)
        send(zs1.at[c, 1], zr1.at[c, 1], t_s.at[c, 1, 0], t_r.at[c, 1, 0], down_z)

    def z_back(c, i):
        for w, dev in ((0, up_z), (1, down_z)):
            target = zmod(HALF - i) if w == 0 else zmod(i - HALF)
            if i == 1:
                landed(zr1.at[c, w], t_r.at[c, w, 0])
                zsn[c, w, 0, w] = (tok[c, target, w] + zr1[c, w].astype(F32)).astype(BF)
                zsn[c, w, 0, 1 - w] = tok[c, target, 1 - w].astype(BF)
            else:
                landed(zrn.at[c, w, i - 2], t_r.at[c, w, i - 1])
                zsn[c, w, i - 1] = (tok[c, target] + zrn[c, w, i - 2].astype(F32)).astype(BF)
            send(zsn.at[c, w, i - 1], zrn.at[c, w, i - 1], t_s.at[c, w, i], t_r.at[c, w, i], dev)

    def finish(c):
        for w in range(2):
            landed(zrn.at[c, w, HALF - 2], t_r.at[c, w, HALF - 1])
        total = tok[c, z] + zrn[c, 0, HALF - 2].astype(F32) + zrn[c, 1, HALF - 2].astype(F32)
        fin[c] = total.astype(BF)
        ig[c, k] = fin[c, k]
        send(fin.at[c, ok], ig.at[c, k], f_s.at[c], f_r.at[c], sibling)

    def adapters_send():
        for o in range(ND):
            flag = jnp.where(slot(xmod(o), j) == first, 1.0, 0.0)
            ad_in[o] = choose(flag, adam_in[0, 0], adam_in[0, 1]).astype(BF)
            ad_out[o] = choose(flag, adam_out[0, 0], adam_out[0, 1]).astype(BF)
            if o:
                send(ad_in.at[o], cin.at[d], a_s.at[o, 0], a_r.at[o, 0], (xmod(o), j))
                send(ad_out.at[o], cout.at[d], a_s.at[o, 1], a_r.at[o, 1], (xmod(o), j))
        cin[d] = ad_in[0]
        cout[d] = ad_out[0]

    def adapters_wait():
        for o in range(1, ND):
            landed(cin.at[xmod(-o)], a_r.at[o, 0])
            landed(cout.at[xmod(-o)], a_r.at[o, 1])

    def grads_send():
        gs_in[...] = (SCALE * dot(lgr[...], hid[...], ((0,), (0,)))).astype(BF).reshape(gs_in.shape)
        for c in range(NC):
            rows_g = xbuf[c, 1].reshape(ALL_ROWS, CC)
            r = SCALE * dot(lin[...], rows_g, ((0,), (0,)))
            gs_out[:, :, c * CC : (c + 1) * CC] = r.astype(BF).reshape(ND, R // ND, CC)
        for o in range(1, ND):
            dev = (xmod(o), j)
            send(gs_in.at[xmod(o)], gr_in.at[o], g_s.at[o, 0], g_r.at[o, 0], dev)
            send(gs_out.at[xmod(o)], gr_out.at[o], g_s.at[o, 1], g_r.at[o, 1], dev)
        gr_in[0] = gs_in[d]
        gr_out[0] = gs_out[d]

    def optimizer():
        for c in adam_loads[2:]:
            c.wait()
        for o in range(1, ND):
            landed(gr_in.at[o], g_r.at[o, 0])
            landed(gr_out.at[o], g_r.at[o, 1])
        for adam, gr, st, mo, va, ss, side in (
            (adam_in, gr_in, st_in, mo_in, va_in, ss_in, 0),
            (adam_out, gr_out, st_out, mo_out, va_out, ss_out, 1),
        ):
            for e in range(2):
                total = jnp.zeros(adam.shape[2:], F32)
                for o in range(ND):
                    flag = jnp.where(slot(xmod(-o), j) == first + e, 1.0, 0.0)
                    total = total + choose(flag, gr[o].astype(F32), jnp.zeros(adam.shape[2:], F32))
                st[e], mo[e], va[e] = adamw(adam[0, e], total, adam[1, e], adam[2, e])
            for o in range(ND):
                flag = jnp.where(slot(xmod(o), j) == first, 1.0, 0.0)
                ss[o] = choose(flag, st[0], st[1]).astype(BF)
                dst = rin if side == 0 else rout
                if o:
                    send(ss.at[o], dst.at[d], s_s.at[o, side], s_r.at[o, side], (xmod(o), j))
                else:
                    dst[d] = ss[0]

    locals_ = {}
    order = [NC] + list(range(NC))
    last = HALF + 4
    for tau in range(len(order) + last):
        for at, c in enumerate(order):
            if 0 <= tau - at <= HALF:
                z_step(c, tau - at)
        if tau == 2:
            for c in adam_loads[:2]:
                c.wait()
            adapters_send()
        if tau == HALF:
            build_pick()
        for c in range(NC):
            phase = tau - (c + 1) - HALF
            if phase == 2:
                x_forward(c)
        for c in range(NC):
            phase = tau - (c + 1) - HALF
            if phase == 1:
                y_wait(c, locals_[c])
        for c in range(NC):
            phase = tau - (c + 1) - HALF
            if phase == 0:
                locals_[c] = select(c)
        if tau == HALF + 1:
            pick_t[...] = pick[...].T
        for c in range(NC):
            phase = tau - (c + 1) - HALF
            if phase == 3:
                if c == 0:
                    for copy in loads:
                        copy.wait()
                    adapters_wait()
                x_wait(c)
                accumulate(c)
    middle()
    for tau in range(NC + HALF + 4):
        for c in range(NC):
            phase = tau - c
            if phase == 0:
                back(c)
        for c in range(NC):
            phase = tau - c
            if phase == 1:
                back_forward(c)
            elif phase == 2:
                locals_[c] = y_back(c)
            elif phase == 3:
                tokens_back(c, locals_[c])
            elif 4 <= phase < 4 + HALF - 1:
                z_back(c, phase - 3)
            elif phase == 4 + HALF - 1:
                finish(c)
        if tau == 1:
            grads_send()
        if tau == 4:
            optimizer()
    for o in range(1, ND):
        landed(rin.at[xmod(-o)], s_r.at[o, 0])
        landed(rout.at[xmod(-o)], s_r.at[o, 1])
    re_in[0] = rin[...].reshape(R, H)
    re_out[0] = rout[...].reshape(R, D)
    for c in range(NC):
        landed(ig.at[c, ok], f_r.at[c])
        for h in range(2):
            ig_out[:, c * CC + h * CH : c * CC + (h + 1) * CH] = ig[c, h]
    for c in sent:
        c.wait_send()


def per_device(
    saved_input, output_grad, route_probs, expert_choice, slot_expert, frozen_gate, frozen_up, frozen_down,
    adapter_in, adapter_out, moment_in, moment_out, second_in, second_out,
):
    T, D = saved_input.shape
    H = frozen_gate.shape[2]
    E, RD = adapter_in.shape[:2]
    R = RD * ND
    CC, CH = D // NC, D // NC // 2
    j = lax.axis_index("expert")
    meta = jnp.concatenate([expert_choice.astype(F32), route_probs], axis=1).T
    place = lax.broadcasted_iota(jnp.int32, (16, 4 * T), 1) // T == j % 4
    meta = jnp.where(place, jnp.tile(meta, (1, 4)), 0.0)
    sem = pltpu.SemaphoreType.DMA
    V = pltpu.VMEM
    scratch = [
        V((D, H), BF), V((D, H), BF), V((H, D), BF),
        V((3, E, RD, H), F32), V((3, E, RD, D), F32),
        V((NC, T, CC), BF), V((NC, NZ, 2, T, CC), BF), V((NZ, 2, 16, 4 * T), F32),
        V((ALL_ROWS, NS * T), BF), V((NS * T, ALL_ROWS), BF), V((ALL_ROWS, 128), F32),
        V((NC, 2 * NY, 2, ROWS, CC), BF), V((NC, 2, NY, ROWS, CC), BF), V((NC, 2, ND, NY, ROWS, CC), BF),
        V((ALL_ROWS, H), F32), V((ALL_ROWS, H), F32), V((ALL_ROWS, H), F32), V((ALL_ROWS, R), F32),
        V((ALL_ROWS, H), BF), V((ALL_ROWS, H), BF), V((ALL_ROWS, H), BF), V((ALL_ROWS, R), BF), V((ALL_ROWS, R), BF),
        V((NC, ND, 2, NY, ROWS, CH), BF), V((NC, 2, NY, ROWS, CH), BF), V((NC, 2, 2, NY, ROWS, CH), BF),
        V((NC, 2, NY, ROWS, CH), BF), V((NC, 2 * NY, 2, ROWS, CH), BF), V((NC, NZ, 2, T, CH), F32),
        V((NC, 2, T, CH), BF), V((NC, 2, T, CH), BF),
        V((NC, 2, HALF - 1, 2, T, CH), BF), V((NC, 2, HALF - 1, 2, T, CH), BF),
        V((NC, 2, T, CH), BF), V((NC, 2, T, CH), BF),
        V((ND, RD, H), BF), V((ND, RD, D), BF), V((ND, RD, H), BF), V((ND, RD, D), BF),
        V((ND, RD, H), BF), V((ND, RD, D), BF), V((ND, RD, H), BF), V((ND, RD, D), BF),
        V((ND, RD, H), BF), V((ND, RD, D), BF), V((ND, RD, H), BF), V((ND, RD, D), BF),
        sem((9,)), sem((NC + 1,)), sem((NC + 1,)), sem((NC + 1, 2, HALF)), sem((NC + 1, 2, HALF)),
        sem((NC, 2 * NY, 2)), sem((NC, NY, 2, 2)), sem((NC, 2)), sem((NC, 4)), sem((NC, 4)),
        sem((ND, 2)), sem((ND, 2)),
        sem((NC, 2)), sem((NC, 2)), sem((NC, 2)), sem((NC, 2)),
        sem((NC, NY, 2, 2)), sem((NC, NY, 2, 2)), sem((NC, 2)),
        sem((NC, 2, HALF)), sem((NC, 2, HALF)), sem((NC,)), sem((NC,)),
        sem((ND, 2)), sem((ND, 2)), sem((ND, 2)), sem((ND, 2)),
    ]
    vm = pl.BlockSpec(memory_space=pltpu.VMEM)
    anyspace = pl.BlockSpec(memory_space=pl.ANY)
    shape = jax.ShapeDtypeStruct
    out_shape = (
        [shape((T, D), BF)]
        + [shape((E, RD, H), F32), shape((E, RD, D), F32)] * 3
        + [shape((1, R, H), BF), shape((1, R, D), BF)]
    )
    return tuple(
        pl.pallas_call(
            kernel,
            out_shape=out_shape,
            in_specs=[vm, vm, vm, pl.BlockSpec(memory_space=pltpu.SMEM)] + [anyspace] * 9,
            out_specs=[vm] * 9,
            scratch_shapes=scratch,
            compiler_params=pltpu.CompilerParams(
                collective_id=0, has_side_effects=True, vmem_limit_bytes=62 * 1024 * 1024
            ),
            name="moe_backward",
        )(
            saved_input, output_grad, meta, slot_expert, frozen_gate, frozen_up, frozen_down,
            adapter_in, adapter_out, moment_in, moment_out, second_in, second_out,
        )
    )


def solution(mesh):
    token, state = P(("dp", "expert"), None), P("expert", "dp", None)
    slot3 = P(("dp", "expert"), None, None)
    return jax.shard_map(
        per_device,
        mesh=mesh,
        in_specs=(token,) * 4 + (P(),) + (slot3,) * 3 + (state,) * 6,
        out_specs=(token,) + (state,) * 6 + (slot3,) * 2,
        check_vma=False,
    )
```

```python
import functools

import jax
import jax.numpy as jnp
from jax import lax
from jax.experimental import pallas as pl
from jax.experimental.pallas import tpu as pltpu
from jax.sharding import PartitionSpec as P

MESH = pl.DeviceIdType.MESH
STEP = 100
SCALE = 2.0
BETA1 = 0.9
BETA2 = 0.999
DECAY = 0.01
EPS = 1e-08
ND, NY, NZ = 4, 4, 8
CAP = 3
NS = 2 * NZ
ROWS = CAP * NS
PLANE = NY * ROWS
ALL_ROWS = ND * PLANE
NC = 4
HALF = NZ // 2
BF = jnp.bfloat16
F32 = jnp.float32


def dot(a, b, dims=((1,), (0,))):
    return lax.dot_general(a, b, (dims, ((), ())), preferred_element_type=F32)


def choose(flag, a, b):
    return jnp.where(jnp.full(a.shape, flag, F32) > 0.5, a, b)


def adamw(param, grad, first, second):
    first_new = BETA1 * first + (1.0 - BETA1) * grad
    second_new = BETA2 * second + (1.0 - BETA2) * grad * grad
    corr_one = 1.0 - BETA1**STEP
    corr_two = 1.0 - BETA2**STEP
    step = first_new / corr_one / (jnp.sqrt(second_new / corr_two) + EPS) + DECAY * param
    return step, first_new, second_new


def kernel(
    x_ref, g_ref, meta_ref, slots_ref, wg_hbm, wu_hbm, wd_hbm, *rest
):
    adam_hbm, rest = rest[:6], rest[6:]
    (ig_out, st_in, st_out, mo_in, mo_out, va_in, va_out, re_in, re_out), rest = rest[:9], rest[9:]
    (
        wg, wu, wd, adam_in, adam_out, stage, zbuf, mbuf, pick, pick_t, weight, sendbuf, xbuf,
        gacc, uacc, hacc, lacc, hid, ugr, ggr, lgr, lin,
        bbuf, r1buf, r2buf, osum, rbuf, zs, zr, fin, ig,
        ad_in, ad_out, cin, cout, gs_in, gs_out, gr_in, gr_out, ss_in, ss_out, rin, rout,
        hbm_sem, sib_s, sib_r, z_s, z_r, y_s, y_r, yl_s, x_s, x_r, a_s, a_r,
        b1_s, b1_r, b2_s, b2_r, q_s, q_r, ql_s, t_s, t_r, f_s, f_r, g_s, g_r, s_s, s_r,
    ) = rest
    D, H = wg.shape
    T = x_ref.shape[0]
    R = cin.shape[0] * cin.shape[1]
    CC = D // NC
    CH = CC // 2
    d = lax.axis_index("dp")
    j = lax.axis_index("expert")
    y = lax.div(j, 2 * NZ)
    z = lax.rem(lax.div(j, 2), NZ)
    k = lax.rem(j, 2)
    ok = 1 - k

    def col(yy, zz, kk):
        return (yy * NZ + zz) * 2 + kk

    def ymod(o):
        return lax.rem(y + o + NY, NY)

    def zmod(o):
        return lax.rem(z + o + NZ, NZ)

    def xmod(o):
        return lax.rem(d + o + ND, ND)

    sibling = (d, col(y, z, ok))
    right, left = (xmod(1), j), (xmod(-1), j)
    up_z, down_z = (d, col(y, zmod(1), k)), (d, col(y, zmod(-1), k))

    sent = []

    def send(src, dst, ss, rs, dev):
        c = pltpu.make_async_remote_copy(
            src_ref=src, dst_ref=dst, send_sem=ss, recv_sem=rs, device_id=dev, device_id_type=MESH
        )
        c.start()
        sent.append(c)

    def landed(dst, rs):
        pltpu.make_async_remote_copy(
            src_ref=dst, dst_ref=dst, send_sem=rs, recv_sem=rs, device_id=sibling, device_id_type=MESH
        ).wait_recv()

    loads = [
        pltpu.make_async_copy(wg_hbm.at[0], wg, hbm_sem.at[0]),
        pltpu.make_async_copy(wu_hbm.at[0], wu, hbm_sem.at[1]),
        pltpu.make_async_copy(wd_hbm.at[0], wd, hbm_sem.at[2]),
    ]
    adam_loads = []
    for i in range(3):
        adam_loads.append(pltpu.make_async_copy(adam_hbm[2 * i], adam_in.at[i], hbm_sem.at[3 + 2 * i]))
        adam_loads.append(pltpu.make_async_copy(adam_hbm[2 * i + 1], adam_out.at[i], hbm_sem.at[4 + 2 * i]))
    for c in adam_loads + loads:
        c.start()

    partners = [sibling] + [(d, col(y, zmod(o), k)) for o in range(1, NZ)]
    partners += [(d, col(ymod(o), z, kk)) for o in range(1, NY) for kk in range(2)]
    partners += [(xmod(o), j) for o in range(1, ND)]
    barrier = pltpu.get_barrier_semaphore()
    for dev in partners:
        pl.semaphore_signal(barrier, inc=1, device_id=dev, device_id_type=MESH)

    @pl.when(k == 0)
    def _():
        for c in range(NC):
            zbuf[c, z, 0] = x_ref[:, c * CC : (c + 1) * CC]
            stage[c] = g_ref[:, c * CC : (c + 1) * CC]

    @pl.when(k == 1)
    def _():
        for c in range(NC):
            zbuf[c, z, 1] = g_ref[:, c * CC : (c + 1) * CC]
            stage[c] = x_ref[:, c * CC : (c + 1) * CC]

    mbuf[z, k] = meta_ref[...]
    pl.semaphore_wait(barrier, len(partners))

    send(meta_ref, mbuf.at[z, k], sib_s.at[NC], sib_r.at[NC], sibling)
    for c in range(NC):
        send(stage.at[c], zbuf.at[c, z, k], sib_s.at[c], sib_r.at[c], sibling)

    def zref(c):
        return mbuf if c == NC else zbuf.at[c]

    far = sorted(range(1, NZ), key=lambda o: -min(o, NZ - o))

    def z_send(c, i):
        buf = zref(c)
        a, b = zmod(1 - i), zmod(i - 1)
        if i < HALF:
            send(buf.at[a], buf.at[a], z_s.at[c, 0, i - 1], z_r.at[c, 0, i - 1], up_z)
            send(buf.at[b], buf.at[b], z_s.at[c, 1, i - 1], z_r.at[c, 1, i - 1], down_z)
        else:
            send(buf.at[a, 0], buf.at[a, 0], z_s.at[c, 0, i - 1], z_r.at[c, 0, i - 1], up_z)
            send(buf.at[b, 1], buf.at[b, 1], z_s.at[c, 1, i - 1], z_r.at[c, 1, i - 1], down_z)

    def z_wait(c, i):
        buf = zref(c)
        a, b = zmod(-i), zmod(i)
        if i < HALF:
            landed(buf.at[a], z_r.at[c, 0, i - 1])
            landed(buf.at[b], z_r.at[c, 1, i - 1])
        else:
            landed(buf.at[a, 0], z_r.at[c, 0, i - 1])
            landed(buf.at[b, 1], z_r.at[c, 1, i - 1])

    def z_step(c, i):
        if i == 0:
            landed(zref(c).at[z, ok], sib_r.at[c])
        else:
            z_wait(c, i)
        if i < HALF:
            z_send(c, i + 1)

    def slot(q, jj):
        return slots_ref[q, jj].astype(F32)

    hosted = slot(d, j)
    first = (2 * j).astype(F32)
    both = (4 * j + 1).astype(F32)

    taken = jnp.float32(1.0)
    for q in range(ND):
        same = jnp.where(slot(q, j) == hosted, 1.0, 0.0)
        taken = taken * jnp.where(q < d, 1.0 - same, 1.0)
    mine = [jnp.float32(1.0)] + [
        taken * jnp.where(both - slot(xmod(-o), j) == hosted, 1.0, 0.0) for o in range(1, ND)
    ]

    def build_pick():
        groups = [
            mbuf[2 * q, 0] + mbuf[2 * q, 1] + mbuf[2 * q + 1, 0] + mbuf[2 * q + 1, 1]
            for q in range(NZ // 2)
        ]
        meta = jnp.concatenate(groups, axis=1)
        width = meta.shape[1]
        row = lax.broadcasted_iota(jnp.int32, (NS, width), 0)
        lane = lax.broadcasted_iota(jnp.int32, (NS, width), 1)
        experts = jnp.zeros((NS, width), F32)
        for o in range(NY):
            for kk in range(2):
                jj = col(ymod(o), z, kk)
                host = slot(d, jj)
                other = (4 * jj + 1).astype(F32) - host
                e = (o * 2 + kk) * 2
                experts = jnp.where(row == e, jnp.full((NS, width), other, F32), experts)
                experts = jnp.where(row == e + 1, jnp.full((NS, width), host, F32), experts)
        hit = jnp.zeros((NS, width), F32)
        prob = jnp.zeros((NS, width), F32)
        for kk in range(8):
            m = jnp.broadcast_to(meta[kk : kk + 1], (NS, width)) == experts
            hit = jnp.where(m, 1.0, hit)
            prob = jnp.where(m, jnp.broadcast_to(meta[8 + kk : 9 + kk], (NS, width)), prob)
        seg = lax.shift_right_logical(lane, 5) == row
        sa = lax.broadcasted_iota(jnp.int32, (width, width), 0)
        sb = lax.broadcasted_iota(jnp.int32, (width, width), 1)
        before = (sa < sb) & (lax.shift_right_logical(sa, 5) == lax.shift_right_logical(sb, 5))
        rank = dot(hit.astype(BF), jnp.where(before, 1.0, 0.0).astype(BF))
        key = jnp.where(hit > 0.5, rank, -1.0)
        unit = jnp.where(k == 0, 1.0, 0.0)
        for e in range(4 * NY):
            for r in range(CAP):
                at = (e * CAP + r) * NS
                m = (jnp.broadcast_to(key[e : e + 1], (NS, width)) == float(r)) & seg
                block = jnp.where(m, 1.0, 0.0)
                pick[pl.ds(at, NS), :] = block.astype(BF)
                total = jnp.sum(block * jnp.broadcast_to(prob[e : e + 1], (NS, width)), axis=1, keepdims=True)
                total = unit + (1.0 - unit) * total
                weight[pl.ds(at, NS), :] = jnp.broadcast_to(total, (NS, weight.shape[1]))

    def select(c):
        tokens = zbuf[c].reshape(NS * T, CC)
        for o in (2, 1, 3, 0):
            for kk in range(2):
                t = o * 2 + kk
                rows = pl.ds(t * 2 * ROWS, 2 * ROWS)
                got = dot(pick[rows, :], tokens)
                w = weight[rows, :]
                got = jnp.concatenate([got[:, i : i + 128] * w for i in range(0, CC, 128)], axis=1)
                sendbuf[c, t] = got.astype(BF).reshape(2, ROWS, CC)
                if o:
                    dev = (d, col(ymod(o), z, kk))
                    send(sendbuf.at[c, t], xbuf.at[c, k, 0:2, o], y_s.at[c, t], y_r.at[c, o, k], dev)
        send(sendbuf.at[c, ok], xbuf.at[c, k, 0:2, 0], y_s.at[c, 0], y_r.at[c, 0, k], sibling)
        own = pltpu.make_async_copy(sendbuf.at[c, k], xbuf.at[c, k, 0:2, 0], yl_s.at[c])
        own.start()
        return own

    def y_wait(c, own):
        for o in range(1, NY):
            for kk in range(2):
                landed(xbuf.at[c, kk, 0:2, o], y_r.at[c, o, kk])
        landed(xbuf.at[c, ok, 0:2, 0], y_r.at[c, 0, ok])
        own.wait()
        send(xbuf.at[c, :, 0], xbuf.at[c, :, 2], x_s.at[c, 0], x_r.at[c, 0], right)
        send(xbuf.at[c, :, 0], xbuf.at[c, :, 4], x_s.at[c, 1], x_r.at[c, 1], left)

    def x_forward(c):
        landed(xbuf.at[c, :, 2], x_r.at[c, 0])
        send(xbuf.at[c, 0, 2], xbuf.at[c, 0, 3], x_s.at[c, 2], x_r.at[c, 2], right)
        landed(xbuf.at[c, :, 4], x_r.at[c, 1])
        send(xbuf.at[c, 1, 4], xbuf.at[c, 1, 3], x_s.at[c, 3], x_r.at[c, 3], left)

    def x_wait(c):
        landed(xbuf.at[c, 0, 3], x_r.at[c, 2])
        landed(xbuf.at[c, 1, 3], x_r.at[c, 3])

    NB = 256

    def accumulate(c):
        def add(acc, cols, value):
            n = value.shape[1]
            for p in range(ND):
                rows = slice(p * PLANE, (p + 1) * PLANE)
                part = value[rows]
                if p:
                    part = choose(mine[p], part, jnp.zeros((PLANE, n), F32))
                if c == 0:
                    acc[rows, cols] = part
                else:
                    acc[rows, cols] += part

        def body(n, carry):
            cols = pl.ds(pl.multiple_of(n * NB, NB), NB)
            rows_x = xbuf[c, 0, 1:].reshape(ALL_ROWS, CC)
            add(gacc, cols, dot(rows_x, wg[c * CC : (c + 1) * CC, cols]))
            add(uacc, cols, dot(rows_x, wu[c * CC : (c + 1) * CC, cols]))
            rows_g = xbuf[c, 1, 1:].reshape(ALL_ROWS, CC)
            add(hacc, cols, dot(rows_g, wd[cols, c * CC : (c + 1) * CC], ((1,), (1,))))
            return carry

        lax.fori_loop(0, H // NB, body, 0)
        rows_g = xbuf[c, 1, 1:].reshape(ALL_ROWS, CC)
        co = cout[:, :, c * CC : (c + 1) * CC].reshape(R, CC)
        add(lacc, slice(0, R), dot(rows_g, co, ((1,), (1,))))

    EB = 96

    def middle():
        ci = cin[...].reshape(R, H)

        def body(n, carry):
            rows = pl.ds(pl.multiple_of(n * EB, EB), EB)
            low = lacc[rows, :].astype(BF)
            lgr[rows, :] = low
            gate, up = gacc[rows, :], uacc[rows, :]
            hg = hacc[rows, :] + SCALE * dot(low, ci)
            sg = jax.nn.sigmoid(gate)
            act = gate * sg
            hidden = (act * up).astype(BF)
            hid[rows, :] = hidden
            ugr[rows, :] = (hg * act).astype(BF)
            ggr[rows, :] = (hg * up * sg * (1.0 + gate * (1.0 - sg))).astype(BF)
            lin[rows, :] = dot(hidden, ci, ((1,), (1,))).astype(BF)
            return carry

        lax.fori_loop(0, ALL_ROWS // EB, body, 0)

    def back(c):
        for h in range(2):
            lo = c * CC + h * CH
            r = dot(ggr[...], wg[lo : lo + CH, :], ((1,), (1,))) + dot(ugr[...], wu[lo : lo + CH, :], ((1,), (1,)))
            r = r.astype(BF).reshape(ND, NY, ROWS, CH)
            for p in range(ND):
                bbuf[c, p, h] = r[p]
        send(bbuf.at[c, 2, 0], r1buf.at[c, 0], b1_s.at[c, 0], b1_r.at[c, 0], right)
        send(bbuf.at[c, 2, 1], r1buf.at[c, 1], b1_s.at[c, 1], b1_r.at[c, 1], left)

    def back_forward(c):
        landed(r1buf.at[c, 0], b1_r.at[c, 0])
        bbuf[c, 3, 0] = bbuf[c, 3, 0] + r1buf[c, 0]
        send(bbuf.at[c, 3], r2buf.at[c, 0], b2_s.at[c, 0], b2_r.at[c, 0], right)
        landed(r1buf.at[c, 1], b1_r.at[c, 1])
        bbuf[c, 1, 1] = bbuf[c, 1, 1] + r1buf[c, 1]
        send(bbuf.at[c, 1], r2buf.at[c, 1], b2_s.at[c, 1], b2_r.at[c, 1], left)

    def rows_back(c, src, i):
        for o in (2, 1, 3):
            for h in range(2):
                dev = (d, col(ymod(-o), z, h))
                send(src(h, o), rbuf.at[c, o * 2 + k, i], q_s.at[c, o, h, i], q_r.at[c, o, k, i], dev)
        send(src(ok, 0), rbuf.at[c, k, i], q_s.at[c, 0, 0, i], q_r.at[c, 0, k, i], sibling)
        own = pltpu.make_async_copy(src(k, 0), rbuf.at[c, k, i], ql_s.at[c, i])
        own.start()
        return own

    def sum_back(c):
        landed(r2buf.at[c, 0], b2_r.at[c, 0])
        landed(r2buf.at[c, 1], b2_r.at[c, 1])
        osum[c] = r2buf[c, 0] + r2buf[c, 1]
        return rows_back(c, lambda h, o: osum.at[c, h, o], 0)

    def tokens_back(c, own):
        for i in (1, 0):
            for o in range(1, NY):
                for kk in range(2):
                    landed(rbuf.at[c, o * 2 + kk, i], q_r.at[c, o, kk, i])
            landed(rbuf.at[c, ok, i], q_r.at[c, 0, ok, i])
            own[i].wait()
        got = dot(pick_t[...], rbuf[c].reshape(ALL_ROWS, CH))
        zs[c] = got.astype(BF).reshape(NZ, 2, T, CH)
        for o in far:
            send(zs.at[c, zmod(o)], zr.at[c, o], t_s.at[c, o], t_r.at[c, o], (d, col(y, zmod(o), k)))

    def finish(c):
        total = zs[c, z].astype(F32)
        for o in far:
            landed(zr.at[c, o], t_r.at[c, o])
        for o in far:
            total = total + zr[c, o].astype(F32)
        fin[c] = total.astype(BF)
        ig[c, k] = fin[c, k]
        send(fin.at[c, ok], ig.at[c, k], f_s.at[c], f_r.at[c], sibling)

    def adapters_send():
        for o in range(ND):
            flag = jnp.where(slot(xmod(o), j) == first, 1.0, 0.0)
            ad_in[o] = choose(flag, adam_in[0, 0], adam_in[0, 1]).astype(BF)
            ad_out[o] = choose(flag, adam_out[0, 0], adam_out[0, 1]).astype(BF)
            if o:
                send(ad_in.at[o], cin.at[d], a_s.at[o, 0], a_r.at[o, 0], (xmod(o), j))
                send(ad_out.at[o], cout.at[d], a_s.at[o, 1], a_r.at[o, 1], (xmod(o), j))
        cin[d] = ad_in[0]
        cout[d] = ad_out[0]

    def adapters_wait():
        for o in range(1, ND):
            landed(cin.at[xmod(-o)], a_r.at[o, 0])
            landed(cout.at[xmod(-o)], a_r.at[o, 1])

    def grads_send():
        gs_in[...] = (SCALE * dot(lgr[...], hid[...], ((0,), (0,)))).astype(BF).reshape(gs_in.shape)
        for c in range(NC):
            rows_g = xbuf[c, 1, 1:].reshape(ALL_ROWS, CC)
            r = SCALE * dot(lin[...], rows_g, ((0,), (0,)))
            gs_out[:, :, c * CC : (c + 1) * CC] = r.astype(BF).reshape(ND, R // ND, CC)
        for o in range(1, ND):
            dev = (xmod(o), j)
            send(gs_in.at[xmod(o)], gr_in.at[o], g_s.at[o, 0], g_r.at[o, 0], dev)
            send(gs_out.at[xmod(o)], gr_out.at[o], g_s.at[o, 1], g_r.at[o, 1], dev)
        gr_in[0] = gs_in[d]
        gr_out[0] = gs_out[d]

    def optimizer():
        for c in adam_loads[2:]:
            c.wait()
        for o in range(1, ND):
            landed(gr_in.at[o], g_r.at[o, 0])
            landed(gr_out.at[o], g_r.at[o, 1])
        for adam, gr, st, mo, va, ss, side in (
            (adam_in, gr_in, st_in, mo_in, va_in, ss_in, 0),
            (adam_out, gr_out, st_out, mo_out, va_out, ss_out, 1),
        ):
            for e in range(2):
                total = jnp.zeros(adam.shape[2:], F32)
                for o in range(ND):
                    flag = jnp.where(slot(xmod(-o), j) == first + e, 1.0, 0.0)
                    total = total + choose(flag, gr[o].astype(F32), jnp.zeros(adam.shape[2:], F32))
                st[e], mo[e], va[e] = adamw(adam[0, e], total, adam[1, e], adam[2, e])
            for o in range(ND):
                flag = jnp.where(slot(xmod(o), j) == first, 1.0, 0.0)
                ss[o] = choose(flag, st[0], st[1]).astype(BF)
                dst = rin if side == 0 else rout
                if o:
                    send(ss.at[o], dst.at[d], s_s.at[o, side], s_r.at[o, side], (xmod(o), j))
                else:
                    dst[d] = ss[0]

    owns = {}
    early, late = {}, {}
    for i in range(HALF + 1):
        early.setdefault(i, []).extend([(NC, i), (0, i)])
    for i in range(HALF + 1):
        early.setdefault(i + 1, []).append((1, i))
    for c in range(2, NC):
        for i in range(HALF + 1):
            (late if i % 2 else early).setdefault(c + 2 + i // 2, []).append((c, i))
    for tau in range(NC + HALF + 3):
        for c, i in early.get(tau, []):
            z_step(c, i)
        if tau == 1:
            for c in adam_loads[:2]:
                c.wait()
            adapters_send()
        if tau == HALF:
            build_pick()
        at = tau - HALF
        if 0 <= at - 1 < NC:
            y_wait(at - 1, owns[at - 1])
        if 0 <= at - 2 < NC:
            x_forward(at - 2)
        if 0 <= at < NC:
            owns[at] = select(at)
        if at == 0:
            pick_t[...] = pick[...].T
        if at == 3:
            for copy in loads:
                copy.wait()
            adapters_wait()
        if 0 <= at - 3 < NC:
            x_wait(at - 3)
            accumulate(at - 3)
        for c, i in late.get(tau, []):
            z_step(c, i)
    middle()
    for tau in range(NC + 4):
        if tau < NC:
            back(tau)
            owns[tau] = [None, rows_back(tau, lambda h, o, c=tau: bbuf.at[c, 0, h, o], 1)]
        if 0 <= tau - 1 < NC:
            back_forward(tau - 1)
        if 0 <= tau - 2 < NC:
            owns[tau - 2][0] = sum_back(tau - 2)
        if 0 <= tau - 3 < NC:
            tokens_back(tau - 3, owns[tau - 3])
        if 0 <= tau - 4 < NC:
            finish(tau - 4)
        if tau == 1:
            grads_send()
        if tau == 5:
            optimizer()
    for o in range(1, ND):
        landed(rin.at[xmod(-o)], s_r.at[o, 0])
        landed(rout.at[xmod(-o)], s_r.at[o, 1])
    re_in[0] = rin[...].reshape(R, H)
    re_out[0] = rout[...].reshape(R, D)
    for c in range(NC):
        landed(ig.at[c, ok], f_r.at[c])
        for h in range(2):
            ig_out[:, c * CC + h * CH : c * CC + (h + 1) * CH] = ig[c, h]
    for c in sent:
        c.wait_send()


def hand_over(*refs):
    n = len(refs) // 2
    for i in range(n):
        refs[n + i][...] = refs[i][...]


def per_device(
    saved_input, output_grad, route_probs, expert_choice, slot_expert, frozen_gate, frozen_up, frozen_down,
    adapter_in, adapter_out, moment_in, moment_out, second_in, second_out,
):
    T, D = saved_input.shape
    H = frozen_gate.shape[2]
    E, RD = adapter_in.shape[:2]
    R = RD * ND
    CC, CH = D // NC, D // NC // 2
    j = lax.axis_index("expert")
    meta = jnp.concatenate([expert_choice.astype(F32), route_probs], axis=1).T
    place = lax.broadcasted_iota(jnp.int32, (16, 4 * T), 1) // T == j % 4
    meta = jnp.where(place, jnp.tile(meta, (1, 4)), 0.0)
    sem = pltpu.SemaphoreType.DMA
    V = pltpu.VMEM
    scratch = [
        V((D, H), BF), V((D, H), BF), V((H, D), BF),
        V((3, E, RD, H), F32), V((3, E, RD, D), F32),
        V((NC, T, CC), BF), V((NC, NZ, 2, T, CC), BF), V((NZ, 2, 16, 4 * T), F32),
        V((ALL_ROWS, NS * T), BF), V((NS * T, ALL_ROWS), BF), V((ALL_ROWS, 128), F32),
        V((NC, 2 * NY, 2, ROWS, CC), BF), V((NC, 2, ND + 1, NY, ROWS, CC), BF),
        V((ALL_ROWS, H), F32), V((ALL_ROWS, H), F32), V((ALL_ROWS, H), F32), V((ALL_ROWS, R), F32),
        V((ALL_ROWS, H), BF), V((ALL_ROWS, H), BF), V((ALL_ROWS, H), BF), V((ALL_ROWS, R), BF), V((ALL_ROWS, R), BF),
        V((NC, ND, 2, NY, ROWS, CH), BF), V((NC, 2, NY, ROWS, CH), BF), V((NC, 2, 2, NY, ROWS, CH), BF),
        V((NC, 2, NY, ROWS, CH), BF), V((NC, 2 * NY, 2, ROWS, CH), BF),
        V((NC, NZ, 2, T, CH), BF), V((NC, NZ, 2, T, CH), BF),
        V((NC, 2, T, CH), BF), V((NC, 2, T, CH), BF),
        V((ND, RD, H), BF), V((ND, RD, D), BF), V((ND, RD, H), BF), V((ND, RD, D), BF),
        V((ND, RD, H), BF), V((ND, RD, D), BF), V((ND, RD, H), BF), V((ND, RD, D), BF),
        V((ND, RD, H), BF), V((ND, RD, D), BF), V((ND, RD, H), BF), V((ND, RD, D), BF),
        sem((9,)), sem((NC + 1,)), sem((NC + 1,)), sem((NC + 1, 2, HALF)), sem((NC + 1, 2, HALF)),
        sem((NC, 2 * NY)), sem((NC, NY, 2)), sem((NC,)), sem((NC, 4)), sem((NC, 4)),
        sem((ND, 2)), sem((ND, 2)),
        sem((NC, 2)), sem((NC, 2)), sem((NC, 2)), sem((NC, 2)),
        sem((NC, NY, 2, 2)), sem((NC, NY, 2, 2)), sem((NC, 2)),
        sem((NC, NZ)), sem((NC, NZ)), sem((NC,)), sem((NC,)),
        sem((ND, 2)), sem((ND, 2)), sem((ND, 2)), sem((ND, 2)),
    ]
    vm = pl.BlockSpec(memory_space=pltpu.VMEM)
    anyspace = pl.BlockSpec(memory_space=pl.ANY)
    shape = jax.ShapeDtypeStruct
    out_shape = (
        [shape((T, D), BF)]
        + [shape((E, RD, H), F32), shape((E, RD, D), F32)] * 3
        + [shape((1, R, H), BF), shape((1, R, D), BF)]
    )
    results = pl.pallas_call(
        kernel,
        out_shape=out_shape,
        in_specs=[vm, vm, vm, pl.BlockSpec(memory_space=pltpu.SMEM)] + [anyspace] * 9,
        out_specs=[vm] * 9,
        scratch_shapes=scratch,
        compiler_params=pltpu.CompilerParams(
            collective_id=0, has_side_effects=True, vmem_limit_bytes=62 * 1024 * 1024
        ),
        name="moe_backward",
    )(
        saved_input, output_grad, meta, slot_expert, frozen_gate, frozen_up, frozen_down,
        adapter_in, adapter_out, moment_in, moment_out, second_in, second_out,
    )
    return tuple(
        pl.pallas_call(
            hand_over,
            out_shape=out_shape,
            in_specs=[vm] * 9,
            out_specs=[vm] * 9,
            name="hand_over",
        )(*results)
    )


def solution(mesh):
    token, state = P(("dp", "expert"), None), P("expert", "dp", None)
    slot3 = P(("dp", "expert"), None, None)
    return jax.shard_map(
        per_device,
        mesh=mesh,
        in_specs=(token,) * 4 + (P(),) + (slot3,) * 3 + (state,) * 6,
        out_specs=(token,) + (state,) * 6 + (slot3,) * 2,
        check_vma=False,
    )
```

```python
import functools

import jax
import jax.numpy as jnp
from jax import lax
from jax.experimental import pallas as pl
from jax.experimental.pallas import tpu as pltpu
from jax.sharding import PartitionSpec as P

MESH = pl.DeviceIdType.MESH
STEP = 100
SCALE = 2.0
BETA1 = 0.9
BETA2 = 0.999
DECAY = 0.01
EPS = 1e-08
ND, NY, NZ = 4, 4, 8
CAP = 3
NS = 2 * NZ
ROWS = CAP * NS
PLANE = NY * ROWS
ALL_ROWS = ND * PLANE
NC = 4
HALF = NZ // 2
BF = jnp.bfloat16
F32 = jnp.float32


def dot(a, b, dims=((1,), (0,))):
    return lax.dot_general(a, b, (dims, ((), ())), preferred_element_type=F32)


def choose(flag, a, b):
    return jnp.where(jnp.full(a.shape, flag, F32) > 0.5, a, b)


def adamw(param, grad, first, second):
    first_new = BETA1 * first + (1.0 - BETA1) * grad
    second_new = BETA2 * second + (1.0 - BETA2) * grad * grad
    corr_one = 1.0 - BETA1**STEP
    corr_two = 1.0 - BETA2**STEP
    step = first_new / corr_one / (jnp.sqrt(second_new / corr_two) + EPS) + DECAY * param
    return step, first_new, second_new


def kernel(
    x_ref, g_ref, meta_ref, slots_ref, wg_hbm, wu_hbm, wd_hbm, *rest
):
    adam_hbm, rest = rest[:6], rest[6:]
    (ig_out, st_in, st_out, mo_in, mo_out, va_in, va_out, re_in, re_out), rest = rest[:9], rest[9:]
    (
        wg, wu, wd, adam_in, adam_out, stage, zbuf, mbuf, pick, pick_t, weight, sendbuf, xbuf,
        gacc, uacc, hacc, lacc, hid, ugr, ggr, lgr, lin,
        bbuf, r1buf, r2buf, osum, rbuf, zs, zr, fin, ig,
        ad_in, ad_out, cin, cout, gs_in, gs_out, gr_in, gr_out, ss_in, ss_out, rin, rout,
        hbm_sem, sib_s, sib_r, z_s, z_r, y_s, y_r, yl_s, x_s, x_r, a_s, a_r,
        b1_s, b1_r, b2_s, b2_r, q_s, q_r, ql_s, t_s, t_r, f_s, f_r, g_s, g_r, s_s, s_r,
    ) = rest
    D, H = wg.shape
    T = x_ref.shape[0]
    R = cin.shape[0] * cin.shape[1]
    CC = D // NC
    CH = CC // 2
    d = lax.axis_index("dp")
    j = lax.axis_index("expert")
    y = lax.div(j, 2 * NZ)
    z = lax.rem(lax.div(j, 2), NZ)
    k = lax.rem(j, 2)
    ok = 1 - k

    def col(yy, zz, kk):
        return (yy * NZ + zz) * 2 + kk

    def ymod(o):
        return lax.rem(y + o + NY, NY)

    def zmod(o):
        return lax.rem(z + o + NZ, NZ)

    def xmod(o):
        return lax.rem(d + o + ND, ND)

    sibling = (d, col(y, z, ok))
    right, left = (xmod(1), j), (xmod(-1), j)
    up_z, down_z = (d, col(y, zmod(1), k)), (d, col(y, zmod(-1), k))

    sent = []

    def send(src, dst, ss, rs, dev):
        c = pltpu.make_async_remote_copy(
            src_ref=src, dst_ref=dst, send_sem=ss, recv_sem=rs, device_id=dev, device_id_type=MESH
        )
        c.start()
        sent.append(c)

    def landed(dst, rs):
        pltpu.make_async_remote_copy(
            src_ref=dst, dst_ref=dst, send_sem=rs, recv_sem=rs, device_id=sibling, device_id_type=MESH
        ).wait_recv()

    loads = [
        pltpu.make_async_copy(wg_hbm.at[0], wg, hbm_sem.at[0]),
        pltpu.make_async_copy(wu_hbm.at[0], wu, hbm_sem.at[1]),
        pltpu.make_async_copy(wd_hbm.at[0], wd, hbm_sem.at[2]),
    ]
    adam_loads = []
    for i in range(3):
        adam_loads.append(pltpu.make_async_copy(adam_hbm[2 * i], adam_in.at[i], hbm_sem.at[3 + 2 * i]))
        adam_loads.append(pltpu.make_async_copy(adam_hbm[2 * i + 1], adam_out.at[i], hbm_sem.at[4 + 2 * i]))
    for c in adam_loads + loads:
        c.start()

    partners = [sibling] + [(d, col(y, zmod(o), k)) for o in range(1, NZ)]
    partners += [(d, col(ymod(o), z, kk)) for o in range(1, NY) for kk in range(2)]
    partners += [(xmod(o), j) for o in range(1, ND)]
    barrier = pltpu.get_barrier_semaphore()
    for dev in partners:
        pl.semaphore_signal(barrier, inc=1, device_id=dev, device_id_type=MESH)

    @pl.when(k == 0)
    def _():
        for c in range(NC):
            zbuf[c, z, 0] = x_ref[:, c * CC : (c + 1) * CC]
            stage[c] = g_ref[:, c * CC : (c + 1) * CC]

    @pl.when(k == 1)
    def _():
        for c in range(NC):
            zbuf[c, z, 1] = g_ref[:, c * CC : (c + 1) * CC]
            stage[c] = x_ref[:, c * CC : (c + 1) * CC]

    mbuf[z, k] = meta_ref[...]
    pl.semaphore_wait(barrier, len(partners))

    send(meta_ref, mbuf.at[z, k], sib_s.at[NC], sib_r.at[NC], sibling)
    for c in range(NC):
        send(stage.at[c], zbuf.at[c, z, k], sib_s.at[c], sib_r.at[c], sibling)

    def zref(c):
        return mbuf if c == NC else zbuf.at[c]

    far = sorted(range(1, NZ), key=lambda o: -min(o, NZ - o))

    def z_send(c, i):
        buf = zref(c)
        a, b = zmod(1 - i), zmod(i - 1)
        if i < HALF:
            send(buf.at[a], buf.at[a], z_s.at[c, 0, i - 1], z_r.at[c, 0, i - 1], up_z)
            send(buf.at[b], buf.at[b], z_s.at[c, 1, i - 1], z_r.at[c, 1, i - 1], down_z)
        else:
            send(buf.at[a, 0], buf.at[a, 0], z_s.at[c, 0, i - 1], z_r.at[c, 0, i - 1], up_z)
            send(buf.at[b, 1], buf.at[b, 1], z_s.at[c, 1, i - 1], z_r.at[c, 1, i - 1], down_z)

    def z_wait(c, i):
        buf = zref(c)
        a, b = zmod(-i), zmod(i)
        if i < HALF:
            landed(buf.at[a], z_r.at[c, 0, i - 1])
            landed(buf.at[b], z_r.at[c, 1, i - 1])
        else:
            landed(buf.at[a, 0], z_r.at[c, 0, i - 1])
            landed(buf.at[b, 1], z_r.at[c, 1, i - 1])

    def z_step(c, i):
        if i == 0:
            landed(zref(c).at[z, ok], sib_r.at[c])
        else:
            z_wait(c, i)
        if i < HALF:
            z_send(c, i + 1)

    def slot(q, jj):
        return slots_ref[q, jj].astype(F32)

    hosted = slot(d, j)
    first = (2 * j).astype(F32)
    both = (4 * j + 1).astype(F32)

    taken = jnp.float32(1.0)
    for q in range(ND):
        same = jnp.where(slot(q, j) == hosted, 1.0, 0.0)
        taken = taken * jnp.where(q < d, 1.0 - same, 1.0)
    mine = [jnp.float32(1.0)] + [
        taken * jnp.where(both - slot(xmod(-o), j) == hosted, 1.0, 0.0) for o in range(1, ND)
    ]

    def build_pick():
        groups = [
            mbuf[2 * q, 0] + mbuf[2 * q, 1] + mbuf[2 * q + 1, 0] + mbuf[2 * q + 1, 1]
            for q in range(NZ // 2)
        ]
        meta = jnp.concatenate(groups, axis=1)
        width = meta.shape[1]
        row = lax.broadcasted_iota(jnp.int32, (NS, width), 0)
        lane = lax.broadcasted_iota(jnp.int32, (NS, width), 1)
        experts = jnp.zeros((NS, width), F32)
        for o in range(NY):
            for kk in range(2):
                jj = col(ymod(o), z, kk)
                host = slot(d, jj)
                other = (4 * jj + 1).astype(F32) - host
                e = (o * 2 + kk) * 2
                experts = jnp.where(row == e, jnp.full((NS, width), other, F32), experts)
                experts = jnp.where(row == e + 1, jnp.full((NS, width), host, F32), experts)
        hit = jnp.zeros((NS, width), F32)
        prob = jnp.zeros((NS, width), F32)
        for kk in range(8):
            m = jnp.broadcast_to(meta[kk : kk + 1], (NS, width)) == experts
            hit = jnp.where(m, 1.0, hit)
            prob = jnp.where(m, jnp.broadcast_to(meta[8 + kk : 9 + kk], (NS, width)), prob)
        seg = lax.shift_right_logical(lane, 5) == row
        sa = lax.broadcasted_iota(jnp.int32, (width, width), 0)
        sb = lax.broadcasted_iota(jnp.int32, (width, width), 1)
        before = (sa < sb) & (lax.shift_right_logical(sa, 5) == lax.shift_right_logical(sb, 5))
        rank = dot(hit.astype(BF), jnp.where(before, 1.0, 0.0).astype(BF))
        key = jnp.where(hit > 0.5, rank, -1.0)
        unit = jnp.where(k == 0, 1.0, 0.0)
        for e in range(4 * NY):
            for r in range(CAP):
                at = (e * CAP + r) * NS
                m = (jnp.broadcast_to(key[e : e + 1], (NS, width)) == float(r)) & seg
                block = jnp.where(m, 1.0, 0.0)
                pick[pl.ds(at, NS), :] = block.astype(BF)
                total = jnp.sum(block * jnp.broadcast_to(prob[e : e + 1], (NS, width)), axis=1, keepdims=True)
                total = unit + (1.0 - unit) * total
                weight[pl.ds(at, NS), :] = jnp.broadcast_to(total, (NS, weight.shape[1]))

    def select(c):
        tokens = zbuf[c].reshape(NS * T, CC)
        for o in (2, 1, 3, 0):
            for kk in range(2):
                t = o * 2 + kk
                rows = pl.ds(t * 2 * ROWS, 2 * ROWS)
                got = dot(pick[rows, :], tokens)
                w = weight[rows, :]
                got = jnp.concatenate([got[:, i : i + 128] * w for i in range(0, CC, 128)], axis=1)
                sendbuf[c, t] = got.astype(BF).reshape(2, ROWS, CC)
                if o:
                    dev = (d, col(ymod(o), z, kk))
                    send(sendbuf.at[c, t], xbuf.at[c, k, 0:2, o], y_s.at[c, t], y_r.at[c, o, k], dev)
        send(sendbuf.at[c, ok], xbuf.at[c, k, 0:2, 0], y_s.at[c, 0], y_r.at[c, 0, k], sibling)
        own = pltpu.make_async_copy(sendbuf.at[c, k], xbuf.at[c, k, 0:2, 0], yl_s.at[c])
        own.start()
        return own

    def y_wait(c, own):
        for o in range(1, NY):
            for kk in range(2):
                landed(xbuf.at[c, kk, 0:2, o], y_r.at[c, o, kk])
        landed(xbuf.at[c, ok, 0:2, 0], y_r.at[c, 0, ok])
        own.wait()
        send(xbuf.at[c, :, 0], xbuf.at[c, :, 2], x_s.at[c, 0], x_r.at[c, 0], right)
        send(xbuf.at[c, :, 0], xbuf.at[c, :, 4], x_s.at[c, 1], x_r.at[c, 1], left)

    def x_forward(c):
        landed(xbuf.at[c, :, 2], x_r.at[c, 0])
        send(xbuf.at[c, 0, 2], xbuf.at[c, 0, 3], x_s.at[c, 2], x_r.at[c, 2], right)
        landed(xbuf.at[c, :, 4], x_r.at[c, 1])
        send(xbuf.at[c, 1, 4], xbuf.at[c, 1, 3], x_s.at[c, 3], x_r.at[c, 3], left)

    def x_wait(c):
        landed(xbuf.at[c, 0, 3], x_r.at[c, 2])
        landed(xbuf.at[c, 1, 3], x_r.at[c, 3])

    NB = 256

    def accumulate(c):
        def add(acc, cols, value):
            n = value.shape[1]
            for p in range(ND):
                rows = slice(p * PLANE, (p + 1) * PLANE)
                part = value[rows]
                if p:
                    part = choose(mine[p], part, jnp.zeros((PLANE, n), F32))
                if c == 0:
                    acc[rows, cols] = part
                else:
                    acc[rows, cols] += part

        def body(n, carry):
            cols = pl.ds(pl.multiple_of(n * NB, NB), NB)
            rows_x = xbuf[c, 0, 1:].reshape(ALL_ROWS, CC)
            add(gacc, cols, dot(rows_x, wg[c * CC : (c + 1) * CC, cols]))
            add(uacc, cols, dot(rows_x, wu[c * CC : (c + 1) * CC, cols]))
            rows_g = xbuf[c, 1, 1:].reshape(ALL_ROWS, CC)
            add(hacc, cols, dot(rows_g, wd[cols, c * CC : (c + 1) * CC], ((1,), (1,))))
            return carry

        lax.fori_loop(0, H // NB, body, 0)
        rows_g = xbuf[c, 1, 1:].reshape(ALL_ROWS, CC)
        co = cout[:, :, c * CC : (c + 1) * CC].reshape(R, CC)
        add(lacc, slice(0, R), dot(rows_g, co, ((1,), (1,))))

    EB = 96

    def middle():
        ci = cin[...].reshape(R, H)

        def body(n, carry):
            rows = pl.ds(pl.multiple_of(n * EB, EB), EB)
            low = lacc[rows, :].astype(BF)
            lgr[rows, :] = low
            gate, up = gacc[rows, :], uacc[rows, :]
            hg = hacc[rows, :] + SCALE * dot(low, ci)
            sg = jax.nn.sigmoid(gate)
            act = gate * sg
            hidden = (act * up).astype(BF)
            hid[rows, :] = hidden
            ugr[rows, :] = (hg * act).astype(BF)
            ggr[rows, :] = (hg * up * sg * (1.0 + gate * (1.0 - sg))).astype(BF)
            lin[rows, :] = dot(hidden, ci, ((1,), (1,))).astype(BF)
            return carry

        lax.fori_loop(0, ALL_ROWS // EB, body, 0)

    def back(c):
        for h in range(2):
            lo = c * CC + h * CH
            r = dot(ggr[...], wg[lo : lo + CH, :], ((1,), (1,))) + dot(ugr[...], wu[lo : lo + CH, :], ((1,), (1,)))
            r = r.astype(BF).reshape(ND, NY, ROWS, CH)
            for p in range(ND):
                bbuf[c, p, h] = r[p]
        send(bbuf.at[c, 2, 0], r1buf.at[c, 0], b1_s.at[c, 0], b1_r.at[c, 0], right)
        send(bbuf.at[c, 2, 1], r1buf.at[c, 1], b1_s.at[c, 1], b1_r.at[c, 1], left)

    def back_forward(c):
        landed(r1buf.at[c, 0], b1_r.at[c, 0])
        bbuf[c, 3, 0] = bbuf[c, 3, 0] + r1buf[c, 0]
        send(bbuf.at[c, 3], r2buf.at[c, 0], b2_s.at[c, 0], b2_r.at[c, 0], right)
        landed(r1buf.at[c, 1], b1_r.at[c, 1])
        bbuf[c, 1, 1] = bbuf[c, 1, 1] + r1buf[c, 1]
        send(bbuf.at[c, 1], r2buf.at[c, 1], b2_s.at[c, 1], b2_r.at[c, 1], left)

    def rows_back(c, src, i):
        for o in (2, 1, 3):
            for h in range(2):
                dev = (d, col(ymod(-o), z, h))
                send(src(h, o), rbuf.at[c, o * 2 + k, i], q_s.at[c, o, h, i], q_r.at[c, o, k, i], dev)
        send(src(ok, 0), rbuf.at[c, k, i], q_s.at[c, 0, 0, i], q_r.at[c, 0, k, i], sibling)
        own = pltpu.make_async_copy(src(k, 0), rbuf.at[c, k, i], ql_s.at[c, i])
        own.start()
        return own

    def sum_back(c):
        landed(r2buf.at[c, 0], b2_r.at[c, 0])
        landed(r2buf.at[c, 1], b2_r.at[c, 1])
        osum[c] = r2buf[c, 0] + r2buf[c, 1]
        return rows_back(c, lambda h, o: osum.at[c, h, o], 0)

    def tokens_back(c, own):
        for i in (1, 0):
            for o in range(1, NY):
                for kk in range(2):
                    landed(rbuf.at[c, o * 2 + kk, i], q_r.at[c, o, kk, i])
            landed(rbuf.at[c, ok, i], q_r.at[c, 0, ok, i])
            own[i].wait()
        got = dot(pick_t[...], rbuf[c].reshape(ALL_ROWS, CH))
        zs[c] = got.astype(BF).reshape(NZ, 2, T, CH)
        for o in far:
            send(zs.at[c, zmod(o)], zr.at[c, o], t_s.at[c, o], t_r.at[c, o], (d, col(y, zmod(o), k)))

    def finish(c):
        total = zs[c, z].astype(F32)
        for o in far:
            landed(zr.at[c, o], t_r.at[c, o])
        for o in far:
            total = total + zr[c, o].astype(F32)
        fin[c] = total.astype(BF)
        ig[c, k] = fin[c, k]
        send(fin.at[c, ok], ig.at[c, k], f_s.at[c], f_r.at[c], sibling)

    def adapters_send():
        for o in range(ND):
            flag = jnp.where(slot(xmod(o), j) == first, 1.0, 0.0)
            ad_in[o] = choose(flag, adam_in[0, 0], adam_in[0, 1]).astype(BF)
            ad_out[o] = choose(flag, adam_out[0, 0], adam_out[0, 1]).astype(BF)
            if o:
                send(ad_in.at[o], cin.at[d], a_s.at[o, 0], a_r.at[o, 0], (xmod(o), j))
                send(ad_out.at[o], cout.at[d], a_s.at[o, 1], a_r.at[o, 1], (xmod(o), j))
        cin[d] = ad_in[0]
        cout[d] = ad_out[0]

    def adapters_wait():
        for o in range(1, ND):
            landed(cin.at[xmod(-o)], a_r.at[o, 0])
            landed(cout.at[xmod(-o)], a_r.at[o, 1])

    def grads_send():
        gs_in[...] = (SCALE * dot(lgr[...], hid[...], ((0,), (0,)))).astype(BF).reshape(gs_in.shape)
        for c in range(NC):
            rows_g = xbuf[c, 1, 1:].reshape(ALL_ROWS, CC)
            r = SCALE * dot(lin[...], rows_g, ((0,), (0,)))
            gs_out[:, :, c * CC : (c + 1) * CC] = r.astype(BF).reshape(ND, R // ND, CC)
        for o in range(1, ND):
            dev = (xmod(o), j)
            send(gs_in.at[xmod(o)], gr_in.at[o], g_s.at[o, 0], g_r.at[o, 0], dev)
            send(gs_out.at[xmod(o)], gr_out.at[o], g_s.at[o, 1], g_r.at[o, 1], dev)
        gr_in[0] = gs_in[d]
        gr_out[0] = gs_out[d]

    def optimizer():
        for c in adam_loads[2:]:
            c.wait()
        for o in range(1, ND):
            landed(gr_in.at[o], g_r.at[o, 0])
            landed(gr_out.at[o], g_r.at[o, 1])
        for adam, gr, st, mo, va, ss, side in (
            (adam_in, gr_in, st_in, mo_in, va_in, ss_in, 0),
            (adam_out, gr_out, st_out, mo_out, va_out, ss_out, 1),
        ):
            for e in range(2):
                total = jnp.zeros(adam.shape[2:], F32)
                for o in range(ND):
                    flag = jnp.where(slot(xmod(-o), j) == first + e, 1.0, 0.0)
                    total = total + choose(flag, gr[o].astype(F32), jnp.zeros(adam.shape[2:], F32))
                st[e], mo[e], va[e] = adamw(adam[0, e], total, adam[1, e], adam[2, e])
            for o in range(ND):
                flag = jnp.where(slot(xmod(o), j) == first, 1.0, 0.0)
                ss[o] = choose(flag, st[0], st[1]).astype(BF)
                dst = rin if side == 0 else rout
                if o:
                    send(ss.at[o], dst.at[d], s_s.at[o, side], s_r.at[o, side], (xmod(o), j))
                else:
                    dst[d] = ss[0]

    owns = {}
    early, late = {}, {}
    for i in range(HALF + 1):
        early.setdefault(i, []).extend([(NC, i), (0, i)])
    for i in range(HALF + 1):
        early.setdefault(i + 1, []).append((1, i))
    for c in range(2, NC):
        for i in range(HALF + 1):
            (late if i % 2 else early).setdefault(c + 2 + i // 2, []).append((c, i))
    for tau in range(NC + HALF + 3):
        for c, i in early.get(tau, []):
            z_step(c, i)
        if tau == 1:
            for c in adam_loads[:2]:
                c.wait()
            adapters_send()
        if tau == HALF:
            build_pick()
        at = tau - HALF
        if 0 <= at < NC:
            owns[at] = select(at)
        if 0 <= at - 1 < NC:
            y_wait(at - 1, owns[at - 1])
        if 0 <= at - 2 < NC:
            x_forward(at - 2)
        if at == 0:
            pick_t[...] = pick[...].T
        if at == 3:
            for copy in loads:
                copy.wait()
            adapters_wait()
        if 0 <= at - 3 < NC:
            x_wait(at - 3)
            accumulate(at - 3)
        for c, i in late.get(tau, []):
            z_step(c, i)
    middle()
    for tau in range(NC + 4):
        if tau < NC:
            back(tau)
            owns[tau] = [None, rows_back(tau, lambda h, o, c=tau: bbuf.at[c, 0, h, o], 1)]
        if 0 <= tau - 1 < NC:
            back_forward(tau - 1)
        if 0 <= tau - 2 < NC:
            owns[tau - 2][0] = sum_back(tau - 2)
        if 0 <= tau - 3 < NC:
            tokens_back(tau - 3, owns[tau - 3])
        if 0 <= tau - 4 < NC:
            finish(tau - 4)
        if tau == 1:
            grads_send()
        if tau == 5:
            optimizer()
    for o in range(1, ND):
        landed(rin.at[xmod(-o)], s_r.at[o, 0])
        landed(rout.at[xmod(-o)], s_r.at[o, 1])
    re_in[0] = rin[...].reshape(R, H)
    re_out[0] = rout[...].reshape(R, D)
    for c in range(NC):
        landed(ig.at[c, ok], f_r.at[c])
        for h in range(2):
            ig_out[:, c * CC + h * CH : c * CC + (h + 1) * CH] = ig[c, h]
    for c in sent:
        c.wait_send()


def hand_over(*refs):
    n = len(refs) // 2
    for i in range(n):
        refs[n + i][...] = refs[i][...]


def per_device(
    saved_input, output_grad, route_probs, expert_choice, slot_expert, frozen_gate, frozen_up, frozen_down,
    adapter_in, adapter_out, moment_in, moment_out, second_in, second_out,
):
    T, D = saved_input.shape
    H = frozen_gate.shape[2]
    E, RD = adapter_in.shape[:2]
    R = RD * ND
    CC, CH = D // NC, D // NC // 2
    j = lax.axis_index("expert")
    meta = jnp.concatenate([expert_choice.astype(F32), route_probs], axis=1).T
    place = lax.broadcasted_iota(jnp.int32, (16, 4 * T), 1) // T == j % 4
    meta = jnp.where(place, jnp.tile(meta, (1, 4)), 0.0)
    sem = pltpu.SemaphoreType.DMA
    V = pltpu.VMEM
    scratch = [
        V((D, H), BF), V((D, H), BF), V((H, D), BF),
        V((3, E, RD, H), F32), V((3, E, RD, D), F32),
        V((NC, T, CC), BF), V((NC, NZ, 2, T, CC), BF), V((NZ, 2, 16, 4 * T), F32),
        V((ALL_ROWS, NS * T), BF), V((NS * T, ALL_ROWS), BF), V((ALL_ROWS, 128), F32),
        V((NC, 2 * NY, 2, ROWS, CC), BF), V((NC, 2, ND + 1, NY, ROWS, CC), BF),
        V((ALL_ROWS, H), F32), V((ALL_ROWS, H), F32), V((ALL_ROWS, H), F32), V((ALL_ROWS, R), F32),
        V((ALL_ROWS, H), BF), V((ALL_ROWS, H), BF), V((ALL_ROWS, H), BF), V((ALL_ROWS, R), BF), V((ALL_ROWS, R), BF),
        V((NC, ND, 2, NY, ROWS, CH), BF), V((NC, 2, NY, ROWS, CH), BF), V((NC, 2, 2, NY, ROWS, CH), BF),
        V((NC, 2, NY, ROWS, CH), BF), V((NC, 2 * NY, 2, ROWS, CH), BF),
        V((NC, NZ, 2, T, CH), BF), V((NC, NZ, 2, T, CH), BF),
        V((NC, 2, T, CH), BF), V((NC, 2, T, CH), BF),
        V((ND, RD, H), BF), V((ND, RD, D), BF), V((ND, RD, H), BF), V((ND, RD, D), BF),
        V((ND, RD, H), BF), V((ND, RD, D), BF), V((ND, RD, H), BF), V((ND, RD, D), BF),
        V((ND, RD, H), BF), V((ND, RD, D), BF), V((ND, RD, H), BF), V((ND, RD, D), BF),
        sem((9,)), sem((NC + 1,)), sem((NC + 1,)), sem((NC + 1, 2, HALF)), sem((NC + 1, 2, HALF)),
        sem((NC, 2 * NY)), sem((NC, NY, 2)), sem((NC,)), sem((NC, 4)), sem((NC, 4)),
        sem((ND, 2)), sem((ND, 2)),
        sem((NC, 2)), sem((NC, 2)), sem((NC, 2)), sem((NC, 2)),
        sem((NC, NY, 2, 2)), sem((NC, NY, 2, 2)), sem((NC, 2)),
        sem((NC, NZ)), sem((NC, NZ)), sem((NC,)), sem((NC,)),
        sem((ND, 2)), sem((ND, 2)), sem((ND, 2)), sem((ND, 2)),
    ]
    vm = pl.BlockSpec(memory_space=pltpu.VMEM)
    anyspace = pl.BlockSpec(memory_space=pl.ANY)
    shape = jax.ShapeDtypeStruct
    out_shape = (
        [shape((T, D), BF)]
        + [shape((E, RD, H), F32), shape((E, RD, D), F32)] * 3
        + [shape((1, R, H), BF), shape((1, R, D), BF)]
    )
    results = pl.pallas_call(
        kernel,
        out_shape=out_shape,
        in_specs=[vm, vm, vm, pl.BlockSpec(memory_space=pltpu.SMEM)] + [anyspace] * 9,
        out_specs=[vm] * 9,
        scratch_shapes=scratch,
        compiler_params=pltpu.CompilerParams(
            collective_id=0, has_side_effects=True, vmem_limit_bytes=62 * 1024 * 1024
        ),
        name="moe_backward",
    )(
        saved_input, output_grad, meta, slot_expert, frozen_gate, frozen_up, frozen_down,
        adapter_in, adapter_out, moment_in, moment_out, second_in, second_out,
    )
    return tuple(
        pl.pallas_call(
            hand_over,
            out_shape=out_shape,
            in_specs=[vm] * 9,
            out_specs=[vm] * 9,
            name="hand_over",
        )(*results)
    )


def solution(mesh):
    token, state = P(("dp", "expert"), None), P("expert", "dp", None)
    slot3 = P(("dp", "expert"), None, None)
    return jax.shard_map(
        per_device,
        mesh=mesh,
        in_specs=(token,) * 4 + (P(),) + (slot3,) * 3 + (state,) * 6,
        out_specs=(token,) + (state,) * 6 + (slot3,) * 2,
        check_vma=False,
    )
```

```python
import functools

import jax
import jax.numpy as jnp
from jax import lax
from jax.experimental import pallas as pl
from jax.experimental.pallas import tpu as pltpu
from jax.sharding import PartitionSpec as P

MESH = pl.DeviceIdType.MESH
STEP = 100
SCALE = 2.0
BETA1 = 0.9
BETA2 = 0.999
DECAY = 0.01
EPS = 1e-08
ND, NY, NZ = 4, 4, 8
CAP = 3
NS = 2 * NZ
ROWS = CAP * NS
PLANE = NY * ROWS
ALL_ROWS = ND * PLANE
NC = 4
HALF = NZ // 2
BF = jnp.bfloat16
F32 = jnp.float32


def dot(a, b, dims=((1,), (0,))):
    return lax.dot_general(a, b, (dims, ((), ())), preferred_element_type=F32)


def choose(flag, a, b):
    return jnp.where(jnp.full(a.shape, flag, F32) > 0.5, a, b)


def adamw(param, grad, first, second):
    first_new = BETA1 * first + (1.0 - BETA1) * grad
    second_new = BETA2 * second + (1.0 - BETA2) * grad * grad
    corr_one = 1.0 - BETA1**STEP
    corr_two = 1.0 - BETA2**STEP
    step = first_new / corr_one / (jnp.sqrt(second_new / corr_two) + EPS) + DECAY * param
    return step, first_new, second_new


def kernel(
    x_ref, g_ref, meta_ref, slots_ref, wg_hbm, wu_hbm, wd_hbm, *rest
):
    adam_hbm, rest = rest[:6], rest[6:]
    (ig_out, st_in, st_out, mo_in, mo_out, va_in, va_out, re_in, re_out), rest = rest[:9], rest[9:]
    (
        wg, wu, wd, adam_in, adam_out, stage, zbuf, mbuf, pick, pick_t, weight, sendbuf, xbuf,
        gacc, uacc, hacc, lacc, hid, ugr, ggr, lgr, lin,
        bbuf, r1buf, r2buf, osum, rbuf, zs, zr, fin, ig,
        ad_in, ad_out, cin, cout, gs_in, gs_out, gr_in, gr_out, ss_in, ss_out, rin, rout,
        hbm_sem, sib_s, sib_r, z_s, z_r, y_s, y_r, yl_s, x_s, x_r, a_s, a_r,
        b1_s, b1_r, b2_s, b2_r, q_s, q_r, ql_s, t_s, t_r, f_s, f_r, g_s, g_r, s_s, s_r,
    ) = rest
    D, H = wg.shape
    T = x_ref.shape[0]
    R = cin.shape[0] * cin.shape[1]
    CC = D // NC
    CH = CC // 2
    d = lax.axis_index("dp")
    j = lax.axis_index("expert")
    y = lax.div(j, 2 * NZ)
    z = lax.rem(lax.div(j, 2), NZ)
    k = lax.rem(j, 2)
    ok = 1 - k

    def col(yy, zz, kk):
        return (yy * NZ + zz) * 2 + kk

    def ymod(o):
        return lax.rem(y + o + NY, NY)

    def zmod(o):
        return lax.rem(z + o + NZ, NZ)

    def xmod(o):
        return lax.rem(d + o + ND, ND)

    sibling = (d, col(y, z, ok))
    right, left = (xmod(1), j), (xmod(-1), j)
    up_z, down_z = (d, col(y, zmod(1), k)), (d, col(y, zmod(-1), k))

    sent = []

    def send(src, dst, ss, rs, dev):
        c = pltpu.make_async_remote_copy(
            src_ref=src, dst_ref=dst, send_sem=ss, recv_sem=rs, device_id=dev, device_id_type=MESH
        )
        c.start()
        sent.append(c)

    def landed(dst, rs):
        pltpu.make_async_remote_copy(
            src_ref=dst, dst_ref=dst, send_sem=rs, recv_sem=rs, device_id=sibling, device_id_type=MESH
        ).wait_recv()

    loads = [
        pltpu.make_async_copy(wg_hbm.at[0], wg, hbm_sem.at[0]),
        pltpu.make_async_copy(wu_hbm.at[0], wu, hbm_sem.at[1]),
        pltpu.make_async_copy(wd_hbm.at[0], wd, hbm_sem.at[2]),
    ]
    adam_loads = []
    for i in range(3):
        adam_loads.append(pltpu.make_async_copy(adam_hbm[2 * i], adam_in.at[i], hbm_sem.at[3 + 2 * i]))
        adam_loads.append(pltpu.make_async_copy(adam_hbm[2 * i + 1], adam_out.at[i], hbm_sem.at[4 + 2 * i]))
    for c in adam_loads + loads:
        c.start()

    partners = [sibling] + [(d, col(y, zmod(o), k)) for o in range(1, NZ)]
    partners += [(d, col(ymod(o), z, kk)) for o in range(1, NY) for kk in range(2)]
    partners += [(xmod(o), j) for o in range(1, ND)]
    barrier = pltpu.get_barrier_semaphore()
    for dev in partners:
        pl.semaphore_signal(barrier, inc=1, device_id=dev, device_id_type=MESH)

    @pl.when(k == 0)
    def _():
        for c in range(NC):
            zbuf[c, z, 0] = x_ref[:, c * CC : (c + 1) * CC]
            stage[c] = g_ref[:, c * CC : (c + 1) * CC]

    @pl.when(k == 1)
    def _():
        for c in range(NC):
            zbuf[c, z, 1] = g_ref[:, c * CC : (c + 1) * CC]
            stage[c] = x_ref[:, c * CC : (c + 1) * CC]

    mbuf[z, k] = meta_ref[...]
    pl.semaphore_wait(barrier, len(partners))

    send(meta_ref, mbuf.at[z, k], sib_s.at[NC], sib_r.at[NC], sibling)
    for c in range(NC):
        send(stage.at[c], zbuf.at[c, z, k], sib_s.at[c], sib_r.at[c], sibling)

    def zref(c):
        return mbuf if c == NC else zbuf.at[c]

    far = sorted(range(1, NZ), key=lambda o: -min(o, NZ - o))

    def z_send(c, i):
        buf = zref(c)
        a, b = zmod(1 - i), zmod(i - 1)
        if i < HALF:
            send(buf.at[a], buf.at[a], z_s.at[c, 0, i - 1], z_r.at[c, 0, i - 1], up_z)
            send(buf.at[b], buf.at[b], z_s.at[c, 1, i - 1], z_r.at[c, 1, i - 1], down_z)
        else:
            send(buf.at[a, 0], buf.at[a, 0], z_s.at[c, 0, i - 1], z_r.at[c, 0, i - 1], up_z)
            send(buf.at[b, 1], buf.at[b, 1], z_s.at[c, 1, i - 1], z_r.at[c, 1, i - 1], down_z)

    def z_wait(c, i):
        buf = zref(c)
        a, b = zmod(-i), zmod(i)
        if i < HALF:
            landed(buf.at[a], z_r.at[c, 0, i - 1])
            landed(buf.at[b], z_r.at[c, 1, i - 1])
        else:
            landed(buf.at[a, 0], z_r.at[c, 0, i - 1])
            landed(buf.at[b, 1], z_r.at[c, 1, i - 1])

    def z_step(c, i):
        if i == 0:
            landed(zref(c).at[z, ok], sib_r.at[c])
        else:
            z_wait(c, i)
        if i < HALF:
            z_send(c, i + 1)

    def slot(q, jj):
        return slots_ref[q, jj].astype(F32)

    hosted = slot(d, j)
    first = (2 * j).astype(F32)
    both = (4 * j + 1).astype(F32)

    taken = jnp.float32(1.0)
    for q in range(ND):
        same = jnp.where(slot(q, j) == hosted, 1.0, 0.0)
        taken = taken * jnp.where(q < d, 1.0 - same, 1.0)
    mine = [jnp.float32(1.0)] + [
        taken * jnp.where(both - slot(xmod(-o), j) == hosted, 1.0, 0.0) for o in range(1, ND)
    ]

    def build_pick():
        groups = [
            mbuf[2 * q, 0] + mbuf[2 * q, 1] + mbuf[2 * q + 1, 0] + mbuf[2 * q + 1, 1]
            for q in range(NZ // 2)
        ]
        meta = jnp.concatenate(groups, axis=1)
        width = meta.shape[1]
        row = lax.broadcasted_iota(jnp.int32, (NS, width), 0)
        lane = lax.broadcasted_iota(jnp.int32, (NS, width), 1)
        experts = jnp.zeros((NS, width), F32)
        for o in range(NY):
            for kk in range(2):
                jj = col(ymod(o), z, kk)
                host = slot(d, jj)
                other = (4 * jj + 1).astype(F32) - host
                e = (o * 2 + kk) * 2
                experts = jnp.where(row == e, jnp.full((NS, width), other, F32), experts)
                experts = jnp.where(row == e + 1, jnp.full((NS, width), host, F32), experts)
        hit = jnp.zeros((NS, width), F32)
        prob = jnp.zeros((NS, width), F32)
        for kk in range(8):
            m = jnp.broadcast_to(meta[kk : kk + 1], (NS, width)) == experts
            hit = jnp.where(m, 1.0, hit)
            prob = jnp.where(m, jnp.broadcast_to(meta[8 + kk : 9 + kk], (NS, width)), prob)
        seg = lax.shift_right_logical(lane, 5) == row
        sa = lax.broadcasted_iota(jnp.int32, (width, width), 0)
        sb = lax.broadcasted_iota(jnp.int32, (width, width), 1)
        before = (sa < sb) & (lax.shift_right_logical(sa, 5) == lax.shift_right_logical(sb, 5))
        rank = dot(hit.astype(BF), jnp.where(before, 1.0, 0.0).astype(BF))
        key = jnp.where(hit > 0.5, rank, -1.0)
        unit = jnp.where(k == 0, 1.0, 0.0)
        for e in range(4 * NY):
            for r in range(CAP):
                at = (e * CAP + r) * NS
                m = (jnp.broadcast_to(key[e : e + 1], (NS, width)) == float(r)) & seg
                block = jnp.where(m, 1.0, 0.0)
                pick[pl.ds(at, NS), :] = block.astype(BF)
                total = jnp.sum(block * jnp.broadcast_to(prob[e : e + 1], (NS, width)), axis=1, keepdims=True)
                total = unit + (1.0 - unit) * total
                weight[pl.ds(at, NS), :] = jnp.broadcast_to(total, (NS, weight.shape[1]))

    def select(c):
        tokens = zbuf[c].reshape(NS * T, CC)
        for o in (2, 1, 3, 0):
            for kk in range(2):
                t = o * 2 + kk
                rows = pl.ds(t * 2 * ROWS, 2 * ROWS)
                got = dot(pick[rows, :], tokens)
                w = weight[rows, :]
                got = jnp.concatenate([got[:, i : i + 128] * w for i in range(0, CC, 128)], axis=1)
                sendbuf[c, t] = got.astype(BF).reshape(2, ROWS, CC)
                if o:
                    dev = (d, col(ymod(o), z, kk))
                    send(sendbuf.at[c, t], xbuf.at[c, k, 0:2, o], y_s.at[c, t], y_r.at[c, o, k], dev)
        send(sendbuf.at[c, ok], xbuf.at[c, k, 0:2, 0], y_s.at[c, 0], y_r.at[c, 0, k], sibling)
        own = pltpu.make_async_copy(sendbuf.at[c, k], xbuf.at[c, k, 0:2, 0], yl_s.at[c])
        own.start()
        return own

    def y_wait(c, own):
        for o in range(1, NY):
            for kk in range(2):
                landed(xbuf.at[c, kk, 0:2, o], y_r.at[c, o, kk])
        landed(xbuf.at[c, ok, 0:2, 0], y_r.at[c, 0, ok])
        own.wait()
        send(xbuf.at[c, :, 0], xbuf.at[c, :, 2], x_s.at[c, 0], x_r.at[c, 0], right)
        send(xbuf.at[c, :, 0], xbuf.at[c, :, 4], x_s.at[c, 1], x_r.at[c, 1], left)

    def x_forward(c):
        landed(xbuf.at[c, :, 2], x_r.at[c, 0])
        send(xbuf.at[c, 0, 2], xbuf.at[c, 0, 3], x_s.at[c, 2], x_r.at[c, 2], right)
        landed(xbuf.at[c, :, 4], x_r.at[c, 1])
        send(xbuf.at[c, 1, 4], xbuf.at[c, 1, 3], x_s.at[c, 3], x_r.at[c, 3], left)

    def x_wait(c):
        landed(xbuf.at[c, 0, 3], x_r.at[c, 2])
        landed(xbuf.at[c, 1, 3], x_r.at[c, 3])

    NB = 256

    def accumulate(c):
        def add(acc, cols, value):
            n = value.shape[1]
            for p in range(ND):
                rows = slice(p * PLANE, (p + 1) * PLANE)
                part = value[rows]
                if p:
                    part = choose(mine[p], part, jnp.zeros((PLANE, n), F32))
                if c == 0:
                    acc[rows, cols] = part
                else:
                    acc[rows, cols] += part

        def body(n, carry):
            cols = pl.ds(pl.multiple_of(n * NB, NB), NB)
            rows_x = xbuf[c, 0, 1:].reshape(ALL_ROWS, CC)
            add(gacc, cols, dot(rows_x, wg[c * CC : (c + 1) * CC, cols]))
            add(uacc, cols, dot(rows_x, wu[c * CC : (c + 1) * CC, cols]))
            rows_g = xbuf[c, 1, 1:].reshape(ALL_ROWS, CC)
            add(hacc, cols, dot(rows_g, wd[cols, c * CC : (c + 1) * CC], ((1,), (1,))))
            return carry

        lax.fori_loop(0, H // NB, body, 0)
        rows_g = xbuf[c, 1, 1:].reshape(ALL_ROWS, CC)
        co = cout[:, :, c * CC : (c + 1) * CC].reshape(R, CC)
        add(lacc, slice(0, R), dot(rows_g, co, ((1,), (1,))))

    EB = 96

    def middle():
        ci = cin[...].reshape(R, H)

        def body(n, carry):
            rows = pl.ds(pl.multiple_of(n * EB, EB), EB)
            low = lacc[rows, :].astype(BF)
            lgr[rows, :] = low
            gate, up = gacc[rows, :], uacc[rows, :]
            hg = hacc[rows, :] + SCALE * dot(low, ci)
            sg = jax.nn.sigmoid(gate)
            act = gate * sg
            hidden = (act * up).astype(BF)
            hid[rows, :] = hidden
            ugr[rows, :] = (hg * act).astype(BF)
            ggr[rows, :] = (hg * up * sg * (1.0 + gate * (1.0 - sg))).astype(BF)
            lin[rows, :] = dot(hidden, ci, ((1,), (1,))).astype(BF)
            return carry

        lax.fori_loop(0, ALL_ROWS // EB, body, 0)

    def back(c):
        for h in range(2):
            lo = c * CC + h * CH
            r = dot(ggr[...], wg[lo : lo + CH, :], ((1,), (1,))) + dot(ugr[...], wu[lo : lo + CH, :], ((1,), (1,)))
            r = r.astype(BF).reshape(ND, NY, ROWS, CH)
            for p in range(ND):
                bbuf[c, p, h] = r[p]
        send(bbuf.at[c, 2, 0], r1buf.at[c, 0], b1_s.at[c, 0], b1_r.at[c, 0], right)
        send(bbuf.at[c, 2, 1], r1buf.at[c, 1], b1_s.at[c, 1], b1_r.at[c, 1], left)

    def back_forward(c):
        landed(r1buf.at[c, 0], b1_r.at[c, 0])
        bbuf[c, 3, 0] = bbuf[c, 3, 0] + r1buf[c, 0]
        send(bbuf.at[c, 3], r2buf.at[c, 0], b2_s.at[c, 0], b2_r.at[c, 0], right)
        landed(r1buf.at[c, 1], b1_r.at[c, 1])
        bbuf[c, 1, 1] = bbuf[c, 1, 1] + r1buf[c, 1]
        send(bbuf.at[c, 1], r2buf.at[c, 1], b2_s.at[c, 1], b2_r.at[c, 1], left)

    def rows_back(c, src, i):
        for o in (2, 1, 3):
            for h in range(2):
                dev = (d, col(ymod(-o), z, h))
                send(src(h, o), rbuf.at[c, o * 2 + k, i], q_s.at[c, o, h, i], q_r.at[c, o, k, i], dev)
        send(src(ok, 0), rbuf.at[c, k, i], q_s.at[c, 0, 0, i], q_r.at[c, 0, k, i], sibling)
        own = pltpu.make_async_copy(src(k, 0), rbuf.at[c, k, i], ql_s.at[c, i])
        own.start()
        return own

    def sum_back(c):
        landed(r2buf.at[c, 0], b2_r.at[c, 0])
        landed(r2buf.at[c, 1], b2_r.at[c, 1])
        osum[c] = r2buf[c, 0] + r2buf[c, 1]
        return rows_back(c, lambda h, o: osum.at[c, h, o], 0)

    def tokens_back(c, own):
        for i in (1, 0):
            for o in range(1, NY):
                for kk in range(2):
                    landed(rbuf.at[c, o * 2 + kk, i], q_r.at[c, o, kk, i])
            landed(rbuf.at[c, ok, i], q_r.at[c, 0, ok, i])
            own[i].wait()
        got = dot(pick_t[...], rbuf[c].reshape(ALL_ROWS, CH))
        zs[c] = got.astype(BF).reshape(NZ, 2, T, CH)
        for o in far:
            send(zs.at[c, zmod(o)], zr.at[c, o], t_s.at[c, o], t_r.at[c, o], (d, col(y, zmod(o), k)))

    def finish(c):
        total = zs[c, z].astype(F32)
        for o in far:
            landed(zr.at[c, o], t_r.at[c, o])
        for o in far:
            total = total + zr[c, o].astype(F32)
        fin[c] = total.astype(BF)
        ig[c, k] = fin[c, k]
        send(fin.at[c, ok], ig.at[c, k], f_s.at[c], f_r.at[c], sibling)

    def adapters_send():
        for o in range(ND):
            flag = jnp.where(slot(xmod(o), j) == first, 1.0, 0.0)
            ad_in[o] = choose(flag, adam_in[0, 0], adam_in[0, 1]).astype(BF)
            ad_out[o] = choose(flag, adam_out[0, 0], adam_out[0, 1]).astype(BF)
            if o:
                send(ad_in.at[o], cin.at[d], a_s.at[o, 0], a_r.at[o, 0], (xmod(o), j))
                send(ad_out.at[o], cout.at[d], a_s.at[o, 1], a_r.at[o, 1], (xmod(o), j))
        cin[d] = ad_in[0]
        cout[d] = ad_out[0]

    def adapters_wait():
        for o in range(1, ND):
            landed(cin.at[xmod(-o)], a_r.at[o, 0])
            landed(cout.at[xmod(-o)], a_r.at[o, 1])

    def grads_send():
        gs_in[...] = (SCALE * dot(lgr[...], hid[...], ((0,), (0,)))).astype(BF).reshape(gs_in.shape)
        for c in range(NC):
            rows_g = xbuf[c, 1, 1:].reshape(ALL_ROWS, CC)
            r = SCALE * dot(lin[...], rows_g, ((0,), (0,)))
            gs_out[:, :, c * CC : (c + 1) * CC] = r.astype(BF).reshape(ND, R // ND, CC)
        for o in range(1, ND):
            dev = (xmod(o), j)
            send(gs_in.at[xmod(o)], gr_in.at[o], g_s.at[o, 0], g_r.at[o, 0], dev)
            send(gs_out.at[xmod(o)], gr_out.at[o], g_s.at[o, 1], g_r.at[o, 1], dev)
        gr_in[0] = gs_in[d]
        gr_out[0] = gs_out[d]

    def optimizer():
        for c in adam_loads[2:]:
            c.wait()
        for o in range(1, ND):
            landed(gr_in.at[o], g_r.at[o, 0])
            landed(gr_out.at[o], g_r.at[o, 1])
        for adam, gr, st, mo, va, ss, side in (
            (adam_in, gr_in, st_in, mo_in, va_in, ss_in, 0),
            (adam_out, gr_out, st_out, mo_out, va_out, ss_out, 1),
        ):
            for e in range(2):
                total = jnp.zeros(adam.shape[2:], F32)
                for o in range(ND):
                    flag = jnp.where(slot(xmod(-o), j) == first + e, 1.0, 0.0)
                    total = total + choose(flag, gr[o].astype(F32), jnp.zeros(adam.shape[2:], F32))
                st[e], mo[e], va[e] = adamw(adam[0, e], total, adam[1, e], adam[2, e])
            for o in range(ND):
                flag = jnp.where(slot(xmod(o), j) == first, 1.0, 0.0)
                ss[o] = choose(flag, st[0], st[1]).astype(BF)
                dst = rin if side == 0 else rout
                if o:
                    send(ss.at[o], dst.at[d], s_s.at[o, side], s_r.at[o, side], (xmod(o), j))
                else:
                    dst[d] = ss[0]

    owns = {}
    early, late = {}, {}
    for i in range(HALF + 1):
        early.setdefault(i, []).extend([(NC, i), (0, i)])
    for i in range(HALF + 1):
        early.setdefault(i + 1, []).append((1, i))
    for c in range(2, NC):
        for i in range(HALF + 1):
            (late if i % 2 else early).setdefault(c + 2 + i // 2, []).append((c, i))
    for tau in range(NC + HALF + 3):
        for c, i in early.get(tau, []):
            z_step(c, i)
        if tau == 1:
            for c in adam_loads[:2]:
                c.wait()
            adapters_send()
        if tau == HALF:
            build_pick()
        at = tau - HALF
        if 0 <= at - 1 < NC:
            y_wait(at - 1, owns[at - 1])
        if 0 <= at - 2 < NC:
            x_forward(at - 2)
        if 0 <= at < NC:
            owns[at] = select(at)
        if at == 0:
            pick_t[...] = pick[...].T
        if at == 3:
            for copy in loads:
                copy.wait()
            adapters_wait()
        if 0 <= at - 3 < NC:
            x_wait(at - 3)
            accumulate(at - 3)
        for c, i in late.get(tau, []):
            z_step(c, i)
    middle()
    for tau in range(NC + 4):
        if tau < NC:
            back(tau)
            owns[tau] = [None, rows_back(tau, lambda h, o, c=tau: bbuf.at[c, 0, h, o], 1)]
        if 0 <= tau - 1 < NC:
            back_forward(tau - 1)
        if 0 <= tau - 3 < NC:
            tokens_back(tau - 3, owns[tau - 3])
        if 0 <= tau - 2 < NC:
            owns[tau - 2][0] = sum_back(tau - 2)
        if 0 <= tau - 4 < NC:
            finish(tau - 4)
        if tau == 1:
            grads_send()
        if tau == 5:
            optimizer()
    for o in range(1, ND):
        landed(rin.at[xmod(-o)], s_r.at[o, 0])
        landed(rout.at[xmod(-o)], s_r.at[o, 1])
    re_in[0] = rin[...].reshape(R, H)
    re_out[0] = rout[...].reshape(R, D)
    for c in range(NC):
        landed(ig.at[c, ok], f_r.at[c])
        for h in range(2):
            ig_out[:, c * CC + h * CH : c * CC + (h + 1) * CH] = ig[c, h]
    for c in sent:
        c.wait_send()


def hand_over(*refs):
    n = len(refs) // 2
    for i in range(n):
        refs[n + i][...] = refs[i][...]


def per_device(
    saved_input, output_grad, route_probs, expert_choice, slot_expert, frozen_gate, frozen_up, frozen_down,
    adapter_in, adapter_out, moment_in, moment_out, second_in, second_out,
):
    T, D = saved_input.shape
    H = frozen_gate.shape[2]
    E, RD = adapter_in.shape[:2]
    R = RD * ND
    CC, CH = D // NC, D // NC // 2
    j = lax.axis_index("expert")
    meta = jnp.concatenate([expert_choice.astype(F32), route_probs], axis=1).T
    place = lax.broadcasted_iota(jnp.int32, (16, 4 * T), 1) // T == j % 4
    meta = jnp.where(place, jnp.tile(meta, (1, 4)), 0.0)
    sem = pltpu.SemaphoreType.DMA
    V = pltpu.VMEM
    scratch = [
        V((D, H), BF), V((D, H), BF), V((H, D), BF),
        V((3, E, RD, H), F32), V((3, E, RD, D), F32),
        V((NC, T, CC), BF), V((NC, NZ, 2, T, CC), BF), V((NZ, 2, 16, 4 * T), F32),
        V((ALL_ROWS, NS * T), BF), V((NS * T, ALL_ROWS), BF), V((ALL_ROWS, 128), F32),
        V((NC, 2 * NY, 2, ROWS, CC), BF), V((NC, 2, ND + 1, NY, ROWS, CC), BF),
        V((ALL_ROWS, H), F32), V((ALL_ROWS, H), F32), V((ALL_ROWS, H), F32), V((ALL_ROWS, R), F32),
        V((ALL_ROWS, H), BF), V((ALL_ROWS, H), BF), V((ALL_ROWS, H), BF), V((ALL_ROWS, R), BF), V((ALL_ROWS, R), BF),
        V((NC, ND, 2, NY, ROWS, CH), BF), V((NC, 2, NY, ROWS, CH), BF), V((NC, 2, 2, NY, ROWS, CH), BF),
        V((NC, 2, NY, ROWS, CH), BF), V((NC, 2 * NY, 2, ROWS, CH), BF),
        V((NC, NZ, 2, T, CH), BF), V((NC, NZ, 2, T, CH), BF),
        V((NC, 2, T, CH), BF), V((NC, 2, T, CH), BF),
        V((ND, RD, H), BF), V((ND, RD, D), BF), V((ND, RD, H), BF), V((ND, RD, D), BF),
        V((ND, RD, H), BF), V((ND, RD, D), BF), V((ND, RD, H), BF), V((ND, RD, D), BF),
        V((ND, RD, H), BF), V((ND, RD, D), BF), V((ND, RD, H), BF), V((ND, RD, D), BF),
        sem((9,)), sem((NC + 1,)), sem((NC + 1,)), sem((NC + 1, 2, HALF)), sem((NC + 1, 2, HALF)),
        sem((NC, 2 * NY)), sem((NC, NY, 2)), sem((NC,)), sem((NC, 4)), sem((NC, 4)),
        sem((ND, 2)), sem((ND, 2)),
        sem((NC, 2)), sem((NC, 2)), sem((NC, 2)), sem((NC, 2)),
        sem((NC, NY, 2, 2)), sem((NC, NY, 2, 2)), sem((NC, 2)),
        sem((NC, NZ)), sem((NC, NZ)), sem((NC,)), sem((NC,)),
        sem((ND, 2)), sem((ND, 2)), sem((ND, 2)), sem((ND, 2)),
    ]
    vm = pl.BlockSpec(memory_space=pltpu.VMEM)
    anyspace = pl.BlockSpec(memory_space=pl.ANY)
    shape = jax.ShapeDtypeStruct
    out_shape = (
        [shape((T, D), BF)]
        + [shape((E, RD, H), F32), shape((E, RD, D), F32)] * 3
        + [shape((1, R, H), BF), shape((1, R, D), BF)]
    )
    results = pl.pallas_call(
        kernel,
        out_shape=out_shape,
        in_specs=[vm, vm, vm, pl.BlockSpec(memory_space=pltpu.SMEM)] + [anyspace] * 9,
        out_specs=[vm] * 9,
        scratch_shapes=scratch,
        compiler_params=pltpu.CompilerParams(
            collective_id=0, has_side_effects=True, vmem_limit_bytes=62 * 1024 * 1024
        ),
        name="moe_backward",
    )(
        saved_input, output_grad, meta, slot_expert, frozen_gate, frozen_up, frozen_down,
        adapter_in, adapter_out, moment_in, moment_out, second_in, second_out,
    )
    return tuple(
        pl.pallas_call(
            hand_over,
            out_shape=out_shape,
            in_specs=[vm] * 9,
            out_specs=[vm] * 9,
            name="hand_over",
        )(*results)
    )


def solution(mesh):
    token, state = P(("dp", "expert"), None), P("expert", "dp", None)
    slot3 = P(("dp", "expert"), None, None)
    return jax.shard_map(
        per_device,
        mesh=mesh,
        in_specs=(token,) * 4 + (P(),) + (slot3,) * 3 + (state,) * 6,
        out_specs=(token,) + (state,) * 6 + (slot3,) * 2,
        check_vma=False,
    )
```
